256 devices in a mesh: dp: 32 (over x, y, z_hi), feat: 8 (over z_lo, core).
Axes of the slice: x: 4, y: 4, z: 8 (z_hi: 2, z_lo: 4; z = z_hi * 4 + z_lo), core: 2. Of those that a mesh axis runs over, the one named last changes fastest.
Arguments:
- embeds: bfloat16 [512, 2048, 128], P('dp', 'feat'), may hold values from -6 to 6
- proj_weight: bfloat16 [2048, 256], P('feat'), may hold values from -0.01171875 to 0.01171875
- hidden_weight: bfloat16 [256, 512], replicated, may hold values from -0.375 to 0.375
- out_weight: bfloat16 [512, 128], replicated, may hold values from -0.25 to 0.25
- cotangent: bfloat16 [512, 2048, 128], P('dp', 'feat'), may hold values from -3 to 3
Outputs:
- embed_grad: bfloat16 [512, 2048, 128], P('dp', 'feat')
- proj_grad: float32 [2048, 256], P('feat', 'dp')
- hidden_grad: float32 [256, 512], P('dp')
- out_grad: float32 [512, 128], P('dp')
The draws below stay inside these ranges and needn't reach their ends.
All inputs are finite; a program needn't handle non-finite values.
Results may differ from the reference program's by a relative error of at most 0.025.
Values may be sent and summed in bfloat16 or wider, within the bound.
A program may use at most 64 MiB of HBM per device.

```python
import math
import jax
import jax.numpy as jnp
from jax import lax

NF = 2048
D = 128
K = 256
H = 512
B_DEV = 16
BATCH = 512
N_FEAT = 8


def steps_of(rng, shape, split, least, high):
    def one(position, shards_of):
        draws = jax.random.uniform(jax.random.fold_in(jax.random.fold_in(rng, 6), position), (shards_of,), jnp.float32, least / len(split), high / len(split))
        return jnp.repeat(jnp.exp(draws), shape[position] // shards_of).reshape((-1,) + (1,) * (len(shape) - position - 1))

    factor_of = one(*split[0])
    for cut in split[1:]:
        factor_of = factor_of * one(*cut)
    return factor_of


def noise(key, extent, width, bound, pieces=(), kind=jnp.bfloat16):
    result = jax.random.normal(key, extent, jnp.float32) * width
    if len(pieces) > 0:
        result = steps_of(key, extent, pieces, -0.22, 0.18) * result
    return jnp.clip(result, min=-bound, max=bound).astype(kind)


def setup_inputs(seed: int = 0) -> dict:
    streams_of = jax.random.split(jax.random.key(seed), 6)
    return {
        "embeds": noise(streams_of[0], (BATCH, NF, D), 1.0, 6.0, ((0, 32), (1, 8))),
        "proj_weight": noise(streams_of[1], (NF, K), (NF * D) ** -0.5, 0.01171875, ((0, 8),)),
        "hidden_weight": noise(streams_of[2], (K, H), K ** -0.5, 0.375),
        "out_weight": noise(streams_of[3], (H, D), H ** -0.5, 0.25),
        "cotangent": noise(streams_of[4], (BATCH, NF, D), 0.5, 3.0, ((0, 32), (1, 8))),
    }


def grouped_sum(left, right, form_in, form_out):
    parts = jnp.einsum(form_in, left, right).astype(jnp.bfloat16)
    return lax.optimization_barrier(jnp.sum(parts.astype(jnp.float32), axis=1)).astype(jnp.bfloat16)

def reference(embeds, proj_weight, hidden_weight, out_weight, cotangent):
    group = NF // N_FEAT
    proj_groups = proj_weight.astype(jnp.float32).reshape(N_FEAT, group, K)

    def block(carry, item):
        emb_block, cot_block = item
        emb_float = emb_block.astype(jnp.float32)
        emb_groups = emb_float.reshape(B_DEV, N_FEAT, group, D)
        mixer = grouped_sum(emb_groups, proj_groups, 'bgfd,gfk->bgdk', None)
        inter = jnp.einsum('bfd,bdk->bfk', emb_float, mixer.astype(jnp.float32)).astype(jnp.bfloat16)
        flat_inter = inter.reshape(-1, K)
        pre = jnp.dot(flat_inter, hidden_weight, preferred_element_type=jnp.float32)
        sig = jax.nn.sigmoid(pre)
        act = (pre * sig).astype(jnp.bfloat16)
        flat_cot = cot_block.reshape(-1, D)
        act_cot = jnp.dot(flat_cot, out_weight.T, preferred_element_type=jnp.float32)
        pre_cot = (act_cot * sig * (1.0 + pre * (1.0 - sig))).astype(jnp.bfloat16)
        out_term = jnp.dot(act.T, flat_cot, preferred_element_type=jnp.float32)
        hidden_term = jnp.dot(flat_inter.T, pre_cot, preferred_element_type=jnp.float32)
        inter_cot = jnp.dot(pre_cot, hidden_weight.T, preferred_element_type=jnp.float32).astype(jnp.bfloat16)
        inter_float = inter_cot.astype(jnp.float32).reshape(B_DEV, NF, K)
        mixer_cot = grouped_sum(emb_groups, inter_float.reshape(B_DEV, N_FEAT, group, K), 'bgfd,bgfk->bgdk', None)
        mixer_cot_float = mixer_cot.astype(jnp.float32)
        grad = (cot_block.astype(jnp.float32) + jnp.einsum('bfk,bdk->bfd', inter_float, mixer.astype(jnp.float32)) + jnp.einsum('fk,bdk->bfd', proj_weight.astype(jnp.float32), mixer_cot_float)).astype(jnp.bfloat16)
        proj_term = jnp.einsum('bfd,bdk->fk', emb_float, mixer_cot_float)
        return ((carry[0] + proj_term, carry[1] + hidden_term, carry[2] + out_term), grad)
    blocks = BATCH // B_DEV
    init = (jnp.zeros((NF, K), jnp.float32), jnp.zeros((K, H), jnp.float32), jnp.zeros((H, D), jnp.float32))
    sums, grads = lax.scan(block, init, (embeds.reshape(blocks, B_DEV, NF, D), cotangent.reshape(blocks, B_DEV, NF, D)))
    mlp_scale = 4.0 / BATCH
    proj_scale = 1.0 / (BATCH * math.sqrt(D))
    return (grads.reshape(BATCH, NF, D), sums[0] * proj_scale, sums[1] * mlp_scale, sums[2] * mlp_scale)
```

```python
import functools
import math

import jax
import jax.numpy as jnp
from jax import lax
from jax.experimental import pallas as pl
from jax.experimental.pallas import tpu as pltpu
from jax.sharding import PartitionSpec as P

MESH = pl.DeviceIdType.MESH
BF = jnp.bfloat16
F32 = jnp.float32

LAG_TOTAL = 4
LAG_SHARE = 8
LAG_MLP = 10
LAG2_FIRST = 12
LAG2_PAIR = 16
LAG2_TOTAL = 20
LAG2_SHARE = 24
LAG2_FINAL = 26


def nn(a, b):
    return lax.dot_general(a, b, (((1,), (0,)), ((), ())), preferred_element_type=F32)


def nt(a, b):
    return lax.dot_general(a, b, (((1,), (1,)), ((), ())), preferred_element_type=F32)


def tn(a, b):
    return lax.dot_general(a, b, (((0,), (0,)), ((), ())), preferred_element_type=F32)


def kernel(
    samples, e_hbm, p_hbm, w1_hbm, w2_hbm, c_hbm,
    eg_hbm, pg_ref, hg_ref, og_ref,
    e_ref, p_ref, w1_ref, w2_ref, c_ref, pt_ref, w1t_ref, w2h_ref,
    part, land_a, chip, land_b, pair, land_c, full,
    gacc, stage, hid_acc, out_acc, proj_acc,
    w_mine, w_buddy, w_chip, w_x, w_xs, w_y, w_ys, w_h, w_hs, w_z,
    p_mine, p_x, p_xs, p_y, p_ys, p_h,
    load_sem, store_sem, ssem, rsem, wss, wrs, pss, prs,
):
    dp, ft = lax.axis_index("dp"), lax.axis_index("feat")
    x, y, hi = dp // 8, (dp // 2) % 4, dp % 2
    z, c = ft // 2, ft % 2
    hub = (z == 1) | (z == 2)
    outer = (z == 0) | (z == 3)
    half = (c + z) % 2
    mine = pl.ds(pl.multiple_of(half * 128, 128), 128)
    other = pl.ds(pl.multiple_of((1 - half) * 128, 128), 128)
    buddy = (dp, z * 2 + 1 - c)
    edge_z = jnp.where(z == 0, 1, jnp.where(z == 1, 0, jnp.where(z == 2, 3, 2)))
    edge = (dp, edge_z * 2 + 1 - c)
    across = (dp, (3 - z) * 2 + 1 - c)
    far = (x * 8 + y * 2 + 1 - hi, ft)
    xs = [(((x + d) % 4) * 8 + y * 2 + hi, ft) for d in (1, 2, 3)]
    ys = [(x * 8 + ((y + d) % 4) * 2 + hi, ft) for d in (1, 2, 3)]
    feats = [(dp, (ft + d) % 8) for d in range(1, 8)]

    barrier = pltpu.get_barrier_semaphore()
    peers = feats + xs + ys + [far]
    for peer in peers:
        pl.semaphore_signal(barrier, inc=1, device_id=peer, device_id_type=MESH)

    loads = [
        pltpu.make_async_copy(src, dst, load_sem.at[i])
        for i, (src, dst) in enumerate(
            ((p_hbm, p_ref), (e_hbm, e_ref), (w1_hbm, w1_ref), (w2_hbm, w2_ref), (c_hbm, c_ref))
        )
    ]
    for load in loads:
        load.start()

    def send(src, dst, s_sem, r_sem, device):
        return pltpu.make_async_remote_copy(
            src_ref=src, dst_ref=dst, send_sem=s_sem, recv_sem=r_sem,
            device_id=device, device_id_type=MESH,
        )

    def to_buddy(q, s):
        return send(part.at[q, s, other], land_a.at[q, s], ssem.at[q, 0], rsem.at[q, s, 0], buddy)

    def to_hub(q, s):
        return send(chip.at[q, s], land_b.at[q, s], ssem.at[q, 1], rsem.at[q, s, 1], edge)

    def to_across(q, s):
        return send(pair.at[q, s], land_c.at[q, s], ssem.at[q, 1], rsem.at[q, s, 2], across)

    def to_outer(q, s):
        ref = full.at[q, s, mine]
        return send(ref, ref, ssem.at[q, 2], rsem.at[q, s, 1], edge)

    def share(q, s):
        ref = full.at[q, s, mine]
        return send(ref, ref, ssem.at[q, 3], rsem.at[q, s, 3], buddy)

    def first(q, s):
        to_buddy(q, s).wait_recv()
        chip[q, s] = (part[q, s, mine].astype(F32) + land_a[q, s].astype(F32)).astype(BF)
        to_hub(q, s).start()

    def paired(q, s):
        to_buddy(q, s).wait_recv()
        to_hub(q, s).wait_recv()
        total = part[q, s, mine].astype(F32) + land_a[q, s].astype(F32) + land_b[q, s].astype(F32)
        pair[q, s] = total.astype(BF)
        to_across(q, s).start()

    def totalled(q, s):
        to_across(q, s).wait_recv()
        full[q, s, mine] = (pair[q, s].astype(F32) + land_c[q, s].astype(F32)).astype(BF)
        to_outer(q, s).start()
        share(q, s).start()

    def shared(q, s):
        to_outer(q, s).wait_recv()
        share(q, s).start()

    loads[0].wait()
    pt_ref[...] = p_ref[...].T
    loads[1].wait()
    pl.semaphore_wait(barrier, len(peers))

    def start_sample(s, carry):
        part[0, s] = nn(pt_ref[...], e_ref[s]).astype(BF)
        to_buddy(0, s).start()
        return carry

    lax.fori_loop(0, samples, start_sample, 0)

    @pl.when(outer)
    def _():
        def body(s, carry):
            first(0, s)
            return carry

        lax.fori_loop(0, samples, body, 0)

    hid_acc[...] = jnp.zeros_like(hid_acc)
    out_acc[...] = jnp.zeros_like(out_acc)
    proj_acc[...] = jnp.zeros_like(proj_acc)
    for load in loads[2:]:
        load.wait()
    w1t_ref[...] = (w1_ref[...].T.astype(F32) * 0.5).astype(BF)
    w2h_ref[...] = (w2_ref[...].astype(F32) * 0.5).astype(BF)

    def mlp(s):
        share(0, s).wait_recv()
        emb, cot, mix = e_ref[s], c_ref[s], full[0, s]
        inter = nt(mix, emb).astype(BF)
        u = nn(w1t_ref[...], inter)
        act_cot = nt(w2h_ref[...], cot)
        t = jnp.tanh(u)
        p = 1.0 + t
        a = u * p
        pre_cot = (act_cot * (p + a * (1.0 - t))).astype(BF)
        out_acc[...] += nn(a.astype(BF), cot)
        hid_acc[...] += nt(inter, pre_cot)
        inter_cot = nn(w1_ref[...], pre_cot).astype(BF)
        part[1, s] = nn(inter_cot, emb).astype(BF)
        to_buddy(1, s).start()
        gacc[s] = cot.astype(F32) + tn(inter_cot, mix)

    def final(s):
        share(1, s).wait_recv()
        mix_cot = full[1, s]
        stage[s] = (gacc[s] + nn(p_ref[...], mix_cot)).astype(BF)
        pltpu.make_async_copy(stage.at[s], eg_hbm.at[s], store_sem).start()
        proj_acc[...] += nt(mix_cot, e_ref[s])

    w_core = send(w_mine.at[:, 1 - c], w_buddy, wss.at[0], wrs.at[0], buddy)
    w_xc = [
        send(w_chip.at[pl.ds(((x + d) % 4) * 4, 4)], w_x.at[d - 1], wss.at[d], wrs.at[d], xs[d - 1])
        for d in (1, 2, 3)
    ]
    w_yc = [
        send(w_xs.at[(y + d) % 4], w_y.at[d - 1], wss.at[3 + d], wrs.at[3 + d], ys[d - 1])
        for d in (1, 2, 3)
    ]
    w_hc = send(w_ys, w_h, wss.at[7], wrs.at[7], far)
    w_zc = [
        send(w_hs, w_z.at[z], wss.at[8 + i], wrs.at[8 + z], feats[i]) for i in range(7)
    ]

    def w_first():
        hid = hid_acc[...].reshape(16, 2, 8, 512)
        hid = jnp.concatenate([hid[..., :256], hid[..., 256:]], axis=2)
        w_mine[..., :256] = hid.astype(BF)
        w_mine[..., 256:] = out_acc[...].reshape(16, 2, 16, 128).astype(BF)
        w_core.start()

    def w_along_x():
        w_core.wait_recv()
        w_chip[...] = (w_mine[:, c].astype(F32) + w_buddy[...].astype(F32)).astype(BF)
        for copy in w_xc:
            copy.start()

    def w_along_y():
        total = w_chip[pl.ds(x * 4, 4)].astype(F32)
        for d in range(3):
            w_xc[d].wait_recv()
            total += w_x[d].astype(F32)
        w_xs[...] = total.astype(BF)
        for copy in w_yc:
            copy.start()

    def w_along_z():
        total = w_xs[y].astype(F32)
        for d in range(3):
            w_yc[d].wait_recv()
            total += w_y[d].astype(F32)
        w_ys[...] = total.astype(BF)

        @pl.when(c != hi)
        def _():
            w_hc.start()

    def w_along_feat():
        @pl.when(c == hi)
        def _():
            w_hc.wait_recv()
            total = (w_ys[...].astype(F32) + w_h[...].astype(F32)).astype(BF)
            w_hs[...] = total
            w_z[z] = total
            for copy in w_zc:
                copy.start()

    def w_last():
        total = jnp.zeros((16, 384), F32)
        for source in range(4):
            @pl.when((z != source) | (c != hi))
            def _():
                send(w_hs, w_z.at[source], wss.at[8], wrs.at[8 + source], buddy).wait_recv()

        for source in range(4):
            total += w_z[source].astype(F32)
        hg_ref[:, :256] = total[:8, :256]
        hg_ref[:, 256:] = total[8:, :256]
        og_ref[...] = total[:, 256:]

    def during(t, start, stop, act):
        @pl.when((t >= start) & (t < stop))
        def _():
            act()

    def step(t, carry):
        def on(lag, who, act):
            @pl.when((t >= lag) & (t < lag + samples) & who)
            def _():
                act(t - lag)

        def once(at, act):
            @pl.when(t == at)
            def _():
                act()

        everyone = t >= 0
        on(0, hub, lambda s: paired(0, s))
        on(LAG_TOTAL, hub, lambda s: totalled(0, s))
        on(LAG_SHARE, outer, lambda s: shared(0, s))
        on(LAG2_FIRST, outer, lambda s: first(1, s))
        on(LAG2_PAIR, hub, lambda s: paired(1, s))
        on(LAG2_TOTAL, hub, lambda s: totalled(1, s))
        on(LAG2_SHARE, outer, lambda s: shared(1, s))
        on(LAG_MLP, everyone, mlp)
        once(samples + LAG_MLP, w_first)
        once(samples + LAG_MLP + 2, w_along_x)
        once(samples + LAG_MLP + 7, w_along_y)
        once(samples + LAG_MLP + 12, w_along_z)
        on(LAG2_FINAL, everyone, final)
        return carry

    lax.fori_loop(0, samples + LAG2_FINAL, step, 0)

    p_xc = [
        send(p_mine.at[pl.ds(((x + d) % 4) * 4, 4)], p_x.at[d - 1], pss.at[d], prs.at[d], xs[d - 1])
        for d in (1, 2, 3)
    ]
    p_yc = [
        send(p_xs.at[(y + d) % 4], p_y.at[d - 1], pss.at[3 + d], prs.at[3 + d], ys[d - 1])
        for d in (1, 2, 3)
    ]
    p_hc = send(p_ys.at[1 - hi], p_h, pss.at[0], prs.at[0], far)
    proj = proj_acc[...].reshape(16, 2, 8, 256)
    proj = jnp.concatenate([proj[..., :128], proj[..., 128:]], axis=2)
    p_mine[...] = proj.astype(BF)
    for copy in p_xc:
        copy.start()
    w_along_feat()
    total = p_mine[pl.ds(x * 4, 4)].astype(F32)
    for d in range(3):
        p_xc[d].wait_recv()
        total += p_x[d].astype(F32)
    p_xs[...] = total.astype(BF)
    for copy in p_yc:
        copy.start()
    w_last()
    total = p_xs[y].astype(F32)
    for d in range(3):
        p_yc[d].wait_recv()
        total += p_y[d].astype(F32)
    p_ys[...] = total.astype(BF)
    p_hc.start()

    for q in range(2):
        everything = [send(chip.at[q], land_b.at[q], ssem.at[q, k], rsem.at[q, 0, 0], buddy) for k in range(4)]
        everything[0].wait_send()
        everything[1].wait_send()
        everything[3].wait_send()

        @pl.when(hub)
        def _():
            everything[2].wait_send()
    for copy in [w_core, *w_xc, *w_yc, *p_xc, *p_yc]:
        copy.wait_send()

    @pl.when(c != hi)
    def _():
        w_hc.wait_send()

    @pl.when(c == hi)
    def _():
        for copy in w_zc:
            copy.wait_send()

    pltpu.make_async_copy(stage, eg_hbm, store_sem).wait()
    p_hc.wait_recv()
    total = p_ys[hi].astype(F32) + p_h[...].astype(F32)
    pg_ref[:, :128] = total[:8]
    pg_ref[:, 128:] = total[8:]
    p_hc.wait_send()


def local(embeds, proj_weight, hidden_weight, out_weight, cotangent):
    n, f, d = embeds.shape
    k = proj_weight.shape[1]
    h = hidden_weight.shape[1]
    dp_count = lax.axis_size("dp")
    mlp_scale = 4.0 / (n * dp_count)
    proj_scale = 1.0 / (n * dp_count * math.sqrt(d))
    vmem = pltpu.VMEM
    dma = pltpu.SemaphoreType.DMA
    anywhere = pl.BlockSpec(memory_space=pl.ANY)
    inside = pl.BlockSpec(memory_space=pltpu.VMEM)
    grad, proj, hid, out = pl.pallas_call(
        functools.partial(kernel, n),
        out_shape=(
            jax.ShapeDtypeStruct((n, f, d), BF),
            jax.ShapeDtypeStruct((8, f), F32),
            jax.ShapeDtypeStruct((8, h), F32),
            jax.ShapeDtypeStruct((16, d), F32),
        ),
        in_specs=[anywhere] * 5,
        out_specs=(anywhere, inside, inside, inside),
        scratch_shapes=[
            vmem((n, f, d), BF), vmem((f, k), BF), vmem((k, h), BF), vmem((h, d), BF), vmem((n, f, d), BF),
            vmem((k, f), BF), vmem((h, k), BF), vmem((h, d), BF),
            vmem((2, n, k, d), BF),
            vmem((2, n, k // 2, d), BF),
            vmem((2, n, k // 2, d), BF),
            vmem((2, n, k // 2, d), BF),
            vmem((2, n, k // 2, d), BF),
            vmem((2, n, k // 2, d), BF),
            vmem((2, n, k, d), BF),
            vmem((n, f, d), F32),
            vmem((n, f, d), BF),
            vmem((k, h), F32), vmem((h, d), F32), vmem((k, f), F32),
            vmem((16, 2, 16, 384), BF), vmem((16, 16, 384), BF), vmem((16, 16, 384), BF),
            vmem((3, 4, 16, 384), BF), vmem((4, 16, 384), BF),
            vmem((3, 16, 384), BF), vmem((16, 384), BF),
            vmem((16, 384), BF), vmem((16, 384), BF), vmem((4, 16, 384), BF),
            vmem((16, 2, 16, 128), BF), vmem((3, 4, 2, 16, 128), BF), vmem((4, 2, 16, 128), BF),
            vmem((3, 2, 16, 128), BF), vmem((2, 16, 128), BF), vmem((16, 128), BF),
            dma((5,)), dma, dma((2, 4)), dma((2, n, 4)),
            dma((15,)), dma((12,)), dma((7,)), dma((7,)),
        ],
        compiler_params=pltpu.CompilerParams(
            collective_id=0, has_side_effects=True, vmem_limit_bytes=40 * 1024 * 1024
        ),
    )(embeds, proj_weight, hidden_weight, out_weight, cotangent)
    return grad, proj.T * proj_scale, hid * mlp_scale, out * mlp_scale


def solution(mesh):
    placed = (P("dp", "feat", None), P("feat", None), P(), P(), P("dp", "feat", None))
    return jax.shard_map(
        local,
        mesh=mesh,
        in_specs=placed,
        out_specs=(P("dp", "feat", None), P("feat", "dp"), P("dp", None), P("dp", None)),
        check_vma=False,
    )
```

```python
import functools
import math

import jax
import jax.numpy as jnp
from jax import lax
from jax.experimental import pallas as pl
from jax.experimental.pallas import tpu as pltpu
from jax.sharding import PartitionSpec as P

MESH = pl.DeviceIdType.MESH
BF = jnp.bfloat16
F32 = jnp.float32

LAG_TOTAL = 2
LAG_SHARE = 4
LAG_MLP = 5
LAG2_FIRST = 6
LAG2_PAIR = 8
LAG2_TOTAL = 10
LAG2_SHARE = 12
LAG2_FINAL = 13


def nn(a, b):
    return lax.dot_general(a, b, (((1,), (0,)), ((), ())), preferred_element_type=F32)


def nt(a, b):
    return lax.dot_general(a, b, (((1,), (1,)), ((), ())), preferred_element_type=F32)


def tn(a, b):
    return lax.dot_general(a, b, (((0,), (0,)), ((), ())), preferred_element_type=F32)


def kernel(
    samples, e_hbm, p_hbm, w1_hbm, w2_hbm, c_hbm,
    eg_any, pg_ref, hg_ref, og_ref,
    e_ref, p_ref, w1_ref, w2_ref, c_ref, pt_ref, w1t_ref, w2h_ref,
    part, land_a, chip, land_b, pair, land_c, full,
    gacc, stage, hid_acc, out_acc, proj_acc,
    w_mine, w_buddy, w_chip, w_xy, w_plane, w_z, w_all,
    p_mine, p_land,
    load_sem, store_sem, ssem, rsem, wss, wrs, pss, prs, relay,
):
    pairs = samples // 2
    dp, ft = lax.axis_index("dp"), lax.axis_index("feat")
    x, y, hi = dp // 8, (dp // 2) % 4, dp % 2
    z, c = ft // 2, ft % 2
    hub = (z == 1) | (z == 2)
    outer = (z == 0) | (z == 3)
    half = (c + z) % 2
    mine = pl.ds(pl.multiple_of(half * 128, 128), 128)
    other = pl.ds(pl.multiple_of((1 - half) * 128, 128), 128)
    buddy = (dp, z * 2 + 1 - c)
    edge_z = jnp.where(z == 0, 1, jnp.where(z == 1, 0, jnp.where(z == 2, 3, 2)))
    edge = (dp, edge_z * 2 + 1 - c)
    across = (dp, (3 - z) * 2 + 1 - c)
    ring = (dp + 1 - 2 * hi, (3 - z) * 2 + c)
    third = (jnp.where(hub, dp, dp + 1 - 2 * hi), (3 - z) * 2 + jnp.where(hub, 1 - c, c))
    sides = [
        (((x + 1) % 4) * 8 + y * 2 + hi, ft),
        (((x + 3) % 4) * 8 + y * 2 + hi, ft),
        (x * 8 + ((y + 1) % 4) * 2 + hi, ft),
        (x * 8 + ((y + 3) % 4) * 2 + hi, ft),
    ]

    barrier = pltpu.get_barrier_semaphore()
    peers = [buddy, edge, third] + sides
    for peer in peers:
        pl.semaphore_signal(barrier, inc=1, device_id=peer, device_id_type=MESH)

    loads = [
        pltpu.make_async_copy(src, dst, load_sem.at[i])
        for i, (src, dst) in enumerate(
            ((p_hbm, p_ref), (e_hbm, e_ref), (w1_hbm, w1_ref), (w2_hbm, w2_ref), (c_hbm, c_ref))
        )
    ]
    for load in loads:
        load.start()

    def tell(r):
        for peer in sides:
            pl.semaphore_signal(relay.at[r], inc=1, device_id=peer, device_id_type=MESH)

    def hear(r):
        pl.semaphore_wait(relay.at[r], 4)

    def tell_ring(r):
        pl.semaphore_signal(relay.at[r], inc=1, device_id=ring, device_id_type=MESH)

    def hear_ring(r):
        pl.semaphore_wait(relay.at[r], 1)

    def send(src, dst, s_sem, r_sem, device):
        return pltpu.make_async_remote_copy(
            src_ref=src, dst_ref=dst, send_sem=s_sem, recv_sem=r_sem,
            device_id=device, device_id_type=MESH,
        )

    def to_buddy(q, s):
        return send(part.at[q, s, other], land_a.at[q, s], ssem.at[q, 0], rsem.at[q, s, 0], buddy)

    def to_hub(q, s):
        return send(chip.at[q, s], land_b.at[q, s], ssem.at[q, 1], rsem.at[q, s, 1], edge)

    def to_across(q, s):
        return send(pair.at[q, s], land_c.at[q, s], ssem.at[q, 1], rsem.at[q, s, 2], across)

    def to_outer(q, s):
        ref = full.at[q, s, mine]
        return send(ref, ref, ssem.at[q, 2], rsem.at[q, s, 1], edge)

    def share(q, s):
        ref = full.at[q, s, mine]
        return send(ref, ref, ssem.at[q, 3], rsem.at[q, s, 3], buddy)

    def first(q, s):
        to_buddy(q, s).wait_recv()
        chip[q, s] = (part[q, s, mine].astype(F32) + land_a[q, s].astype(F32)).astype(BF)
        to_hub(q, s).start()

    def paired(q, s):
        to_buddy(q, s).wait_recv()
        to_hub(q, s).wait_recv()
        total = part[q, s, mine].astype(F32) + land_a[q, s].astype(F32) + land_b[q, s].astype(F32)
        pair[q, s] = total.astype(BF)
        to_across(q, s).start()

    def totalled(q, s):
        to_across(q, s).wait_recv()
        full[q, s, mine] = (pair[q, s].astype(F32) + land_c[q, s].astype(F32)).astype(BF)
        to_outer(q, s).start()
        share(q, s).start()

    def shared(q, s):
        to_outer(q, s).wait_recv()
        share(q, s).start()

    loads[0].wait()
    pt_ref[...] = p_ref[...].T
    loads[1].wait()
    pl.semaphore_wait(barrier, len(peers))
    tell(0)

    def start_samples(i, carry):
        for s in [4 * i + j for j in range(4)]:
            part[0, s] = nn(pt_ref[...], e_ref[s]).astype(BF)
        for s in [4 * i + j for j in range(4)]:
            to_buddy(0, s).start()
        return carry

    lax.fori_loop(0, samples // 4, start_samples, 0)

    def first_samples(low, high):
        def body(s, carry):
            first(0, s)
            return carry

        lax.fori_loop(low, high, body, 0)

    @pl.when(outer)
    def _():
        for r in range(3):
            first_samples(4 * r, 4 * r + 4)
            hear(r)
            if r < 2:
                tell(r + 1)
        first_samples(12, samples)

    hid_acc[...] = jnp.zeros_like(hid_acc)
    out_acc[...] = jnp.zeros_like(out_acc)
    proj_acc[...] = jnp.zeros_like(proj_acc)
    for load in loads[2:]:
        load.wait()
    w1t_ref[...] = (w1_ref[...].T.astype(F32) * 0.5).astype(BF)
    w2h_ref[...] = (w2_ref[...].astype(F32) * 0.5).astype(BF)

    def mlp(both):
        for s in both:
            share(0, s).wait_recv()
        emb = [e_ref[s] for s in both]
        cot = [c_ref[s] for s in both]
        mix = [full[0, s] for s in both]
        inter = [nt(m, e).astype(BF) for m, e in zip(mix, emb)]
        u = [nn(w1t_ref[...], v) for v in inter]
        act_cot = [nt(w2h_ref[...], v) for v in cot]
        act, pre_cot = [], []
        for v, g in zip(u, act_cot):
            t = jnp.tanh(v)
            p = 1.0 + t
            a = v * p
            act.append(a.astype(BF))
            pre_cot.append((g * (p + a * (1.0 - t))).astype(BF))
        inter_cot = [nn(w1_ref[...], v).astype(BF) for v in pre_cot]
        for s, v, e in zip(both, inter_cot, emb):
            part[1, s] = nn(v, e).astype(BF)
        out_acc[...] += sum(nn(a, v) for a, v in zip(act, cot))
        hid_acc[...] += sum(nt(v, g) for v, g in zip(inter, pre_cot))
        for s, v, m, g in zip(both, inter_cot, mix, cot):
            gacc[s] = g.astype(F32) + tn(v, m)
        for s in both:
            to_buddy(1, s).start()

    def grad_of(both):
        for s in both:
            stage[s] = (gacc[s] + nn(p_ref[...], full[1, s])).astype(BF)
            pltpu.make_async_copy(stage.at[s], eg_any.at[s], store_sem).start()

    def proj_of(both):
        for s in both:
            share(1, s).wait_recv()
        return sum(nt(full[1, s], e_ref[s]) for s in both)

    def final(both):
        proj_acc[...] += proj_of(both)
        grad_of(both)

    w_core = send(w_mine.at[:, 1 - c], w_buddy, wss.at[0], wrs.at[0], buddy)
    place = x * 4 + y
    w_xyc = []
    for d in range(1, 16):
        there = (place + d) % 16
        w_xyc.append(send(w_chip.at[there], w_xy.at[d], wss.at[1], wrs.at[1], (there * 2 + hi, ft)))
    w_xy_all = send(w_chip.at[pl.ds(0, 15)], w_xy.at[pl.ds(1, 15)], wss.at[1], wrs.at[1], buddy)
    slot = hi * 4 + z
    w_zc = [
        send(w_plane, w_z.at[slot], wss.at[2], wrs.at[2], (place * 2 + c, ((z + d) % 4) * 2 + c))
        for d in range(4)
    ]

    def w_z_some(count):
        return send(w_z.at[pl.ds(0, count)], w_z.at[pl.ds(0, count)], wss.at[2], wrs.at[2], buddy)

    w_last = send(w_all, w_all, wss.at[3], wrs.at[3], buddy)

    def w_first():
        hid = hid_acc[...].reshape(16, 2, 8, 512)
        hid = jnp.concatenate([hid[..., :256], hid[..., 256:]], axis=2)
        w_mine[..., :256] = hid.astype(BF)
        w_mine[..., 256:] = out_acc[...].reshape(16, 2, 16, 128).astype(BF)
        w_core.start()

    def w_along_xy():
        w_core.wait_recv()
        w_chip[...] = (w_mine[:, c].astype(F32) + w_buddy[...].astype(F32)).astype(BF)
        for copy in w_xyc:
            copy.start()

    def w_along_z():
        w_xy_all.wait_recv()
        total = w_chip[place].astype(F32)
        for d in range(1, 16):
            total += w_xy[d].astype(F32)
        w_plane[...] = total.astype(BF)
        for copy in w_zc[1:]:
            copy.start()

        @pl.when(c != hi)
        def _():
            w_zc[0].start()

        @pl.when(c == hi)
        def _():
            w_z[slot] = total.astype(BF)

    def w_share():
        @pl.when(c == hi)
        def _():
            w_z_some(7).wait_recv()
            total = w_z[0].astype(F32)
            for d in range(1, 8):
                total += w_z[d].astype(F32)
            w_all[...] = total
            w_last.start()

    def step(t, carry):
        def on(lag, who, act, count=pairs):
            @pl.when((t >= lag) & (t < lag + count) & who)
            def _():
                s = (t - lag) * 2
                act([s, s + 1])

        def each(act):
            def run(both):
                for s in both:
                    act(s)

            return run

        def once(at, who, act):
            @pl.when((t == at) & who)
            def _():
                act()

        def pass_on(r):
            hear(r)
            if r < 2:
                tell(r + 1)

        everyone = t >= 0
        for r in range(3):
            once(2 * r, hub, functools.partial(pass_on, r))
        on(0, hub, each(functools.partial(paired, 0)))
        on(LAG_TOTAL, hub, each(functools.partial(totalled, 0)))
        on(LAG_SHARE, outer, each(functools.partial(shared, 0)))
        on(LAG_MLP, everyone, mlp)
        once(LAG_MLP + pairs, everyone, w_first)
        once(LAG_MLP, outer, lambda: tell_ring(3))
        once(LAG_MLP + pairs - 2, outer, lambda: tell_ring(4))
        once(LAG2_FIRST, outer, lambda: hear_ring(3))
        once(LAG2_FIRST + pairs - 2, outer, lambda: hear_ring(4))
        on(LAG2_FIRST, outer, each(functools.partial(first, 1)))
        on(LAG2_PAIR, hub, each(functools.partial(paired, 1)))
        on(LAG2_TOTAL, hub, each(functools.partial(totalled, 1)))
        on(LAG2_SHARE, outer, each(functools.partial(shared, 1)))
        once(LAG_MLP + pairs + 1, everyone, w_along_xy)
        once(LAG_MLP + pairs + 6, everyone, w_along_z)
        on(LAG2_FINAL, everyone, final, pairs - 1)
        return carry

    lax.fori_loop(0, pairs - 1 + LAG2_FINAL, step, 0)

    last = [samples - 2, samples - 1]
    proj = (proj_acc[...] + proj_of(last)).reshape(32, 8, 256)
    proj = jnp.concatenate([proj[..., :128], proj[..., 128:]], axis=1)
    p_mine[...] = proj.astype(BF)
    p_copies = []
    for d in range(1, 32):
        there = (dp + d) % 32
        p_copies.append(send(p_mine.at[there], p_land.at[d], pss, prs, (there, ft)))
    for copy in p_copies:
        copy.start()
    p_all = send(p_mine.at[pl.ds(0, 31)], p_land.at[pl.ds(1, 31)], pss, prs, buddy)
    grad_of(last)
    w_share()

    for q in range(2):
        sent = [send(chip.at[q], land_b.at[q], ssem.at[q, k], rsem.at[q, 0, 0], buddy) for k in range(4)]
        for k in (0, 1, 3):
            sent[k].wait_send()

        @pl.when(hub)
        def _():
            sent[2].wait_send()
    w_core.wait_send()
    w_xy_all.wait_send()

    @pl.when(c != hi)
    def _():
        w_z_some(4).wait_send()
        w_last.wait_recv()

    @pl.when(c == hi)
    def _():
        w_z_some(3).wait_send()
        w_last.wait_send()

    hg_ref[:, :256] = w_all[:8, :256]
    hg_ref[:, 256:] = w_all[8:, :256]
    og_ref[...] = w_all[:, 256:]
    pltpu.make_async_copy(stage, eg_any, store_sem).wait()
    p_all.wait_recv()
    total = p_mine[dp].astype(F32)
    for d in range(1, 32):
        total += p_land[d].astype(F32)
    pg_ref[:, :128] = total[:8]
    pg_ref[:, 128:] = total[8:]
    p_all.wait_send()


def finish(scales, eg_in, pg_in, hg_in, og_in, eg_out, pg_out, hg_out, og_out, sem):
    rows = eg_in.shape[0] // 4
    copies = [
        pltpu.make_async_copy(eg_in.at[pl.ds(i * rows, rows)], eg_out.at[pl.ds(i * rows, rows)], sem.at[i])
        for i in range(4)
    ]
    for copy in copies:
        copy.start()
    pg_out[...] = pg_in[...] * scales[0]
    hg_out[...] = hg_in[...] * scales[1]
    og_out[...] = og_in[...] * scales[1]
    for copy in copies:
        copy.wait()


def local(embeds, proj_weight, hidden_weight, out_weight, cotangent):
    n, f, d = embeds.shape
    k = proj_weight.shape[1]
    h = hidden_weight.shape[1]
    dp_count = lax.axis_size("dp")
    mlp_scale = 4.0 / (n * dp_count)
    proj_scale = 1.0 / (n * dp_count * math.sqrt(d))
    vmem = pltpu.VMEM
    dma = pltpu.SemaphoreType.DMA
    hbm = pl.BlockSpec(memory_space=pltpu.HBM)
    anywhere = pl.BlockSpec(memory_space=pl.ANY)
    inside = pl.BlockSpec(memory_space=pltpu.VMEM)
    shapes = (
        jax.ShapeDtypeStruct((n, f, d), BF),
        jax.ShapeDtypeStruct((8, f), F32),
        jax.ShapeDtypeStruct((8, h), F32),
        jax.ShapeDtypeStruct((16, d), F32),
    )
    results = pl.pallas_call(
        functools.partial(kernel, n),
        out_shape=shapes,
        in_specs=[hbm] * 5,
        out_specs=(anywhere, inside, inside, inside),
        scratch_shapes=[
            vmem((n, f, d), BF), vmem((f, k), BF), vmem((k, h), BF), vmem((h, d), BF), vmem((n, f, d), BF),
            vmem((k, f), BF), vmem((h, k), BF), vmem((h, d), BF),
            vmem((2, n, k, d), BF),
            vmem((2, n, k // 2, d), BF),
            vmem((2, n, k // 2, d), BF),
            vmem((2, n, k // 2, d), BF),
            vmem((2, n, k // 2, d), BF),
            vmem((2, n, k // 2, d), BF),
            vmem((2, n, k, d), BF),
            vmem((n, f, d), F32),
            vmem((n, f, d), BF),
            vmem((k, h), F32), vmem((h, d), F32), vmem((k, f), F32),
            vmem((16, 2, 16, 384), BF), vmem((16, 16, 384), BF), vmem((16, 16, 384), BF),
            vmem((16, 16, 384), BF), vmem((16, 384), BF), vmem((8, 16, 384), BF), vmem((16, 384), F32),
            vmem((32, 16, 128), BF), vmem((32, 16, 128), BF),
            dma((5,)), dma, dma((2, 4)), dma((2, n, 4)),
            dma((4,)), dma((4,)), dma, dma, pltpu.SemaphoreType.REGULAR((5,)),
        ],
        compiler_params=pltpu.CompilerParams(
            collective_id=0, has_side_effects=True, vmem_limit_bytes=40 * 1024 * 1024
        ),
    )(embeds, proj_weight, hidden_weight, out_weight, cotangent)
    grad, proj, hid, out = pl.pallas_call(
        functools.partial(finish, (proj_scale, mlp_scale)),
        out_shape=shapes,
        in_specs=[anywhere, inside, inside, inside],
        out_specs=(hbm, inside, inside, inside),
        scratch_shapes=[dma((4,))],
    )(*results)
    return grad, proj.T, hid, out


def solution(mesh):
    placed = (P("dp", "feat", None), P("feat", None), P(), P(), P("dp", "feat", None))
    return jax.shard_map(
        local,
        mesh=mesh,
        in_specs=placed,
        out_specs=(P("dp", "feat", None), P("feat", "dp"), P("dp", None), P("dp", None)),
        check_vma=False,
    )
```

```python
import functools
import math

import jax
import jax.numpy as jnp
from jax import lax
from jax.experimental import pallas as pl
from jax.experimental.pallas import tpu as pltpu
from jax.sharding import PartitionSpec as P

MESH = pl.DeviceIdType.MESH
BF = jnp.bfloat16
F32 = jnp.float32

LAG_TOTAL = 2
LAG_SHARE = 4
LAG_MLP = 5
LAG2_FIRST = 6
LAG2_PAIR = 8
LAG2_TOTAL = 10
LAG2_SHARE = 12
LAG2_FINAL = 13


def nn(a, b):
    return lax.dot_general(a, b, (((1,), (0,)), ((), ())), preferred_element_type=F32)


def nt(a, b):
    return lax.dot_general(a, b, (((1,), (1,)), ((), ())), preferred_element_type=F32)


def tn(a, b):
    return lax.dot_general(a, b, (((0,), (0,)), ((), ())), preferred_element_type=F32)


def kernel(
    samples, proj_scale, mlp_scale, e_hbm, p_hbm, w1_hbm, w2_hbm, c_hbm,
    eg_any, pg_ref, hg_ref, og_ref,
    e_ref, p_ref, w1_ref, w2_ref, c_ref, pt_ref, w1t_ref, w2h_ref,
    part, land_a, chip, land_b, pair, land_c, full,
    gacc, stage, hid_acc, out_acc, proj_acc,
    w_mine, w_buddy, w_chip, w_xy, w_plane, w_z, w_all,
    p_mine, p_land,
    load_sem, store_sem, ssem, rsem, wss, wrs, pss, prs, relay,
):
    pairs = samples // 2
    dp, ft = lax.axis_index("dp"), lax.axis_index("feat")
    x, y, hi = dp // 8, (dp // 2) % 4, dp % 2
    z, c = ft // 2, ft % 2
    hub = (z == 1) | (z == 2)
    outer = (z == 0) | (z == 3)
    half = (c + z) % 2
    mine = pl.ds(pl.multiple_of(half * 128, 128), 128)
    other = pl.ds(pl.multiple_of((1 - half) * 128, 128), 128)
    buddy = (dp, z * 2 + 1 - c)
    edge_z = jnp.where(z == 0, 1, jnp.where(z == 1, 0, jnp.where(z == 2, 3, 2)))
    edge = (dp, edge_z * 2 + 1 - c)
    across = (dp, (3 - z) * 2 + 1 - c)
    ring = (dp + 1 - 2 * hi, (3 - z) * 2 + c)
    third = (jnp.where(hub, dp, dp + 1 - 2 * hi), (3 - z) * 2 + jnp.where(hub, 1 - c, c))
    sides = [
        (((x + 1) % 4) * 8 + y * 2 + hi, ft),
        (((x + 3) % 4) * 8 + y * 2 + hi, ft),
        (x * 8 + ((y + 1) % 4) * 2 + hi, ft),
        (x * 8 + ((y + 3) % 4) * 2 + hi, ft),
    ]

    barrier = pltpu.get_barrier_semaphore()
    peers = [buddy, edge, third] + sides
    for peer in peers:
        pl.semaphore_signal(barrier, inc=1, device_id=peer, device_id_type=MESH)

    loads = [
        pltpu.make_async_copy(src, dst, load_sem.at[i])
        for i, (src, dst) in enumerate(
            ((p_hbm, p_ref), (e_hbm, e_ref), (w1_hbm, w1_ref), (w2_hbm, w2_ref), (c_hbm, c_ref))
        )
    ]
    for load in loads:
        load.start()

    def tell(r):
        for peer in sides:
            pl.semaphore_signal(relay.at[r], inc=1, device_id=peer, device_id_type=MESH)

    def hear(r):
        pl.semaphore_wait(relay.at[r], 4)

    def tell_ring(r):
        pl.semaphore_signal(relay.at[r], inc=1, device_id=ring, device_id_type=MESH)

    def hear_ring(r):
        pl.semaphore_wait(relay.at[r], 1)

    def send(src, dst, s_sem, r_sem, device):
        return pltpu.make_async_remote_copy(
            src_ref=src, dst_ref=dst, send_sem=s_sem, recv_sem=r_sem,
            device_id=device, device_id_type=MESH,
        )

    def to_buddy(q, s):
        return send(part.at[q, s, other], land_a.at[q, s], ssem.at[q, 0], rsem.at[q, s, 0], buddy)

    def to_hub(q, s):
        return send(chip.at[q, s], land_b.at[q, s], ssem.at[q, 1], rsem.at[q, s, 1], edge)

    def to_across(q, s):
        return send(pair.at[q, s], land_c.at[q, s], ssem.at[q, 1], rsem.at[q, s, 2], across)

    def to_outer(q, s):
        ref = full.at[q, s, mine]
        return send(ref, ref, ssem.at[q, 2], rsem.at[q, s, 1], edge)

    def share(q, s):
        ref = full.at[q, s, mine]
        return send(ref, ref, ssem.at[q, 3], rsem.at[q, s, 3], buddy)

    def first(q, s):
        to_buddy(q, s).wait_recv()
        chip[q, s] = (part[q, s, mine].astype(F32) + land_a[q, s].astype(F32)).astype(BF)
        to_hub(q, s).start()

    def paired(q, s):
        to_buddy(q, s).wait_recv()
        to_hub(q, s).wait_recv()
        total = part[q, s, mine].astype(F32) + land_a[q, s].astype(F32) + land_b[q, s].astype(F32)
        pair[q, s] = total.astype(BF)
        to_across(q, s).start()

    def totalled(q, s):
        to_across(q, s).wait_recv()
        full[q, s, mine] = (pair[q, s].astype(F32) + land_c[q, s].astype(F32)).astype(BF)
        to_outer(q, s).start()
        share(q, s).start()

    def shared(q, s):
        to_outer(q, s).wait_recv()
        share(q, s).start()

    loads[0].wait()
    pt_ref[...] = p_ref[...].T
    loads[1].wait()
    pl.semaphore_wait(barrier, len(peers))
    tell(0)

    def start_samples(i, carry):
        for s in [4 * i + j for j in range(4)]:
            part[0, s] = nn(pt_ref[...], e_ref[s]).astype(BF)
        for s in [4 * i + j for j in range(4)]:
            to_buddy(0, s).start()
        return carry

    lax.fori_loop(0, samples // 4, start_samples, 0)

    def first_samples(low, high):
        def body(s, carry):
            first(0, s)
            return carry

        lax.fori_loop(low, high, body, 0)

    @pl.when(outer)
    def _():
        for r in range(3):
            first_samples(4 * r, 4 * r + 4)
            hear(r)
            if r < 2:
                tell(r + 1)
        first_samples(12, samples)

    hid_acc[...] = jnp.zeros_like(hid_acc)
    out_acc[...] = jnp.zeros_like(out_acc)
    proj_acc[...] = jnp.zeros_like(proj_acc)
    for load in loads[2:]:
        load.wait()
    w1t_ref[...] = (w1_ref[...].T.astype(F32) * 0.5).astype(BF)
    w2h_ref[...] = (w2_ref[...].astype(F32) * 0.5).astype(BF)

    def mlp(both):
        for s in both:
            share(0, s).wait_recv()
        emb = [e_ref[s] for s in both]
        cot = [c_ref[s] for s in both]
        mix = [full[0, s] for s in both]
        inter = [nt(m, e).astype(BF) for m, e in zip(mix, emb)]
        u = [nn(w1t_ref[...], v) for v in inter]
        act_cot = [nt(w2h_ref[...], v) for v in cot]
        act, pre_cot = [], []
        for v, g in zip(u, act_cot):
            t = jnp.tanh(v)
            p = 1.0 + t
            a = v * p
            act.append(a.astype(BF))
            pre_cot.append((g * (p + a * (1.0 - t))).astype(BF))
        inter_cot = [nn(w1_ref[...], v).astype(BF) for v in pre_cot]
        for s, v, e in zip(both, inter_cot, emb):
            part[1, s] = nn(v, e).astype(BF)
        out_acc[...] += sum(nn(a, v) for a, v in zip(act, cot))
        hid_acc[...] += sum(nt(v, g) for v, g in zip(inter, pre_cot))
        for s, v, m, g in zip(both, inter_cot, mix, cot):
            gacc[s] = g.astype(F32) + tn(v, m)
        for s in both:
            to_buddy(1, s).start()

    def grad_of(both):
        for s in both:
            stage[s] = (gacc[s] + nn(p_ref[...], full[1, s])).astype(BF)
            pltpu.make_async_copy(stage.at[s], eg_any.at[s], store_sem).start()

    def proj_of(both):
        for s in both:
            share(1, s).wait_recv()
        return sum(nt(full[1, s], e_ref[s]) for s in both)

    def final(both):
        proj_acc[...] += proj_of(both)
        grad_of(both)

    w_core = send(w_mine.at[:, 1 - c], w_buddy, wss.at[0], wrs.at[0], buddy)
    place = x * 4 + y
    w_xyc = []
    for d in range(1, 16):
        there = (place + d) % 16
        w_xyc.append(send(w_chip.at[there], w_xy.at[d], wss.at[1], wrs.at[1], (there * 2 + hi, ft)))
    w_xy_all = send(w_chip.at[pl.ds(0, 15)], w_xy.at[pl.ds(1, 15)], wss.at[1], wrs.at[1], buddy)
    slot = hi * 4 + z
    w_zc = [
        send(w_plane, w_z.at[slot], wss.at[2], wrs.at[2], (place * 2 + c, ((z + d) % 4) * 2 + c))
        for d in range(4)
    ]

    def w_z_some(count):
        return send(w_z.at[pl.ds(0, count)], w_z.at[pl.ds(0, count)], wss.at[2], wrs.at[2], buddy)

    w_last = send(w_all, w_all, wss.at[3], wrs.at[3], buddy)

    def w_first():
        hid = hid_acc[...].reshape(16, 2, 8, 512)
        hid = jnp.concatenate([hid[..., :256], hid[..., 256:]], axis=2)
        w_mine[..., :256] = hid.astype(BF)
        w_mine[..., 256:] = out_acc[...].reshape(16, 2, 16, 128).astype(BF)
        w_core.start()

    def w_along_xy():
        w_core.wait_recv()
        w_chip[...] = (w_mine[:, c].astype(F32) + w_buddy[...].astype(F32)).astype(BF)
        for copy in w_xyc:
            copy.start()

    def w_along_z():
        w_xy_all.wait_recv()
        total = w_chip[place].astype(F32)
        for d in range(1, 16):
            total += w_xy[d].astype(F32)
        w_plane[...] = total.astype(BF)
        for copy in w_zc[1:]:
            copy.start()

        @pl.when(c != hi)
        def _():
            w_zc[0].start()

        @pl.when(c == hi)
        def _():
            w_z[slot] = total.astype(BF)

    def w_share():
        @pl.when(c == hi)
        def _():
            w_z_some(7).wait_recv()
            total = w_z[0].astype(F32)
            for d in range(1, 8):
                total += w_z[d].astype(F32)
            w_all[...] = total
            w_last.start()

    def step(t, carry):
        def on(lag, who, act, count=pairs):
            @pl.when((t >= lag) & (t < lag + count) & who)
            def _():
                s = (t - lag) * 2
                act([s, s + 1])

        def each(act):
            def run(both):
                for s in both:
                    act(s)

            return run

        def once(at, who, act):
            @pl.when((t == at) & who)
            def _():
                act()

        def pass_on(r):
            hear(r)
            if r < 2:
                tell(r + 1)

        everyone = t >= 0
        for r in range(3):
            once(2 * r, hub, functools.partial(pass_on, r))
        on(0, hub, each(functools.partial(paired, 0)))
        on(LAG_TOTAL, hub, each(functools.partial(totalled, 0)))
        on(LAG_SHARE, outer, each(functools.partial(shared, 0)))
        on(LAG_MLP, everyone, mlp)
        once(LAG_MLP + pairs, everyone, w_first)
        once(LAG_MLP, outer, lambda: tell_ring(3))
        once(LAG_MLP + pairs - 2, outer, lambda: tell_ring(4))
        once(LAG2_FIRST, outer, lambda: hear_ring(3))
        once(LAG2_FIRST + pairs - 2, outer, lambda: hear_ring(4))
        on(LAG2_FIRST, outer, each(functools.partial(first, 1)))
        on(LAG2_PAIR, hub, each(functools.partial(paired, 1)))
        on(LAG2_TOTAL, hub, each(functools.partial(totalled, 1)))
        on(LAG2_SHARE, outer, each(functools.partial(shared, 1)))
        once(LAG_MLP + pairs + 1, everyone, w_along_xy)
        once(LAG_MLP + pairs + 6, everyone, w_along_z)
        on(LAG2_FINAL, everyone, final, pairs - 1)
        return carry

    lax.fori_loop(0, pairs - 1 + LAG2_FINAL, step, 0)

    last = [samples - 2, samples - 1]
    proj = (proj_acc[...] + proj_of(last)).reshape(32, 8, 256)
    proj = jnp.concatenate([proj[..., :128], proj[..., 128:]], axis=1)
    p_mine[...] = proj.astype(BF)
    p_copies = []
    for d in range(1, 32):
        there = (dp + d) % 32
        p_copies.append(send(p_mine.at[there], p_land.at[d], pss, prs, (there, ft)))
    for copy in p_copies:
        copy.start()
    p_all = send(p_mine.at[pl.ds(0, 31)], p_land.at[pl.ds(1, 31)], pss, prs, buddy)
    grad_of(last)
    w_share()

    for q in range(2):
        sent = [send(chip.at[q], land_b.at[q], ssem.at[q, k], rsem.at[q, 0, 0], buddy) for k in range(4)]
        for k in (0, 1, 3):
            sent[k].wait_send()

        @pl.when(hub)
        def _():
            sent[2].wait_send()
    w_core.wait_send()
    w_xy_all.wait_send()

    @pl.when(c != hi)
    def _():
        w_z_some(4).wait_send()
        w_last.wait_recv()

    @pl.when(c == hi)
    def _():
        w_z_some(3).wait_send()
        w_last.wait_send()

    hg_ref[:, :256] = w_all[:8, :256] * mlp_scale
    hg_ref[:, 256:] = w_all[8:, :256] * mlp_scale
    og_ref[...] = w_all[:, 256:] * mlp_scale
    pltpu.make_async_copy(stage, eg_any, store_sem).wait()
    p_all.wait_recv()
    total = p_mine[dp].astype(F32)
    for d in range(1, 32):
        total += p_land[d].astype(F32)
    pg_ref[:, :128] = total[:8] * proj_scale
    pg_ref[:, 128:] = total[8:] * proj_scale
    p_all.wait_send()


def finish(eg_in, pg_in, hg_in, og_in, eg_out, pg_out, hg_out, og_out, eg, pg, hg, og, in_sem, out_sem):
    parts = in_sem.shape[0] - 3
    rows = eg.shape[0] // parts
    moves = [(pg_in, pg, pg_out), (hg_in, hg, hg_out), (og_in, og, og_out)]
    for i in range(parts):
        some = pl.ds(i * rows, rows)
        moves.append((eg_in.at[some], eg.at[some], eg_out.at[some]))
    loads = [pltpu.make_async_copy(m[0], m[1], in_sem.at[i]) for i, m in enumerate(moves)]
    stores = [pltpu.make_async_copy(m[1], m[2], out_sem.at[i]) for i, m in enumerate(moves)]
    for load in loads:
        load.start()
    for load, store in zip(loads, stores):
        load.wait()
        store.start()
    for store in stores:
        store.wait()


def local(embeds, proj_weight, hidden_weight, out_weight, cotangent):
    n, f, d = embeds.shape
    k = proj_weight.shape[1]
    h = hidden_weight.shape[1]
    dp_count = lax.axis_size("dp")
    mlp_scale = 4.0 / (n * dp_count)
    proj_scale = 1.0 / (n * dp_count * math.sqrt(d))
    vmem = pltpu.VMEM
    dma = pltpu.SemaphoreType.DMA
    hbm = pl.BlockSpec(memory_space=pltpu.HBM)
    anywhere = pl.BlockSpec(memory_space=pl.ANY)
    inside = pl.BlockSpec(memory_space=pltpu.VMEM)
    shapes = (
        jax.ShapeDtypeStruct((n, f, d), BF),
        jax.ShapeDtypeStruct((8, f), F32),
        jax.ShapeDtypeStruct((8, h), F32),
        jax.ShapeDtypeStruct((16, d), F32),
    )
    results = pl.pallas_call(
        functools.partial(kernel, n, proj_scale, mlp_scale),
        out_shape=shapes,
        in_specs=[hbm] * 5,
        out_specs=(anywhere, inside, inside, inside),
        scratch_shapes=[
            vmem((n, f, d), BF), vmem((f, k), BF), vmem((k, h), BF), vmem((h, d), BF), vmem((n, f, d), BF),
            vmem((k, f), BF), vmem((h, k), BF), vmem((h, d), BF),
            vmem((2, n, k, d), BF),
            vmem((2, n, k // 2, d), BF),
            vmem((2, n, k // 2, d), BF),
            vmem((2, n, k // 2, d), BF),
            vmem((2, n, k // 2, d), BF),
            vmem((2, n, k // 2, d), BF),
            vmem((2, n, k, d), BF),
            vmem((n, f, d), F32),
            vmem((n, f, d), BF),
            vmem((k, h), F32), vmem((h, d), F32), vmem((k, f), F32),
            vmem((16, 2, 16, 384), BF), vmem((16, 16, 384), BF), vmem((16, 16, 384), BF),
            vmem((16, 16, 384), BF), vmem((16, 384), BF), vmem((8, 16, 384), BF), vmem((16, 384), F32),
            vmem((32, 16, 128), BF), vmem((32, 16, 128), BF),
            dma((5,)), dma, dma((2, 4)), dma((2, n, 4)),
            dma((4,)), dma((4,)), dma, dma, pltpu.SemaphoreType.REGULAR((5,)),
        ],
        compiler_params=pltpu.CompilerParams(
            collective_id=0, has_side_effects=True, vmem_limit_bytes=60 * 1024 * 1024
        ),
    )(embeds, proj_weight, hidden_weight, out_weight, cotangent)
    grad, proj, hid, out = pl.pallas_call(
        finish,
        out_shape=shapes,
        in_specs=[hbm] * 4,
        out_specs=(hbm,) * 4,
        scratch_shapes=[vmem(v.shape, v.dtype) for v in shapes] + [dma((7,)), dma((7,))],
        compiler_params=pltpu.CompilerParams(vmem_limit_bytes=60 * 1024 * 1024),
    )(*results)
    return grad, proj.T, hid, out


def solution(mesh):
    placed = (P("dp", "feat", None), P("feat", None), P(), P(), P("dp", "feat", None))
    return jax.shard_map(
        local,
        mesh=mesh,
        in_specs=placed,
        out_specs=(P("dp", "feat", None), P("feat", "dp"), P("dp", None), P("dp", None)),
        check_vma=False,
    )
```

```python
import functools
import itertools
import math

import jax
import jax.numpy as jnp
from jax import lax
from jax.experimental import pallas as pl
from jax.experimental.pallas import tpu as pltpu
from jax.sharding import PartitionSpec as P

MESH = pl.DeviceIdType.MESH
BF = jnp.bfloat16
F32 = jnp.float32

LAG_TOTAL = 5
LAG_SHARE = 10
LAG_MLP = 12
LAG2_FIRST = 15
LAG2_PAIR = 20
LAG2_TOTAL = 25
LAG2_SHARE = 30


def nn(a, b):
    return lax.dot_general(a, b, (((1,), (0,)), ((), ())), preferred_element_type=F32)


def nt(a, b):
    return lax.dot_general(a, b, (((1,), (1,)), ((), ())), preferred_element_type=F32)


def tn(a, b):
    return lax.dot_general(a, b, (((0,), (0,)), ((), ())), preferred_element_type=F32)


def kernel(
    samples, proj_scale, mlp_scale, e_hbm, p_hbm, w1_hbm, w2_hbm, c_hbm,
    eg_any, pg_ref, hg_ref, og_ref,
    e_ref, p_ref, w1_ref, w2_ref, c_ref, pt_ref, w1t_ref, w2h_ref,
    part, land_a, chip, land_b, pair, land_c, full,
    act_cot, icot, inters, acts, pre_cots, stage, hid_acc, out_acc, proj_acc,
    w_mine, w_buddy, w_chip, w_xy, w_plane, w_z, w_all,
    p_mine, p_land,
    e2_ref, load_sem, store_sem, ssem, rsem, wss, wrs, pss, prs, relay,
):
    pairs = samples // 2
    dp, ft = lax.axis_index("dp"), lax.axis_index("feat")
    x, y, hi = dp // 8, (dp // 2) % 4, dp % 2
    z, c = ft // 2, ft % 2
    hub = (z == 1) | (z == 2)
    outer = (z == 0) | (z == 3)
    half = (c + z) % 2
    hi_half = dp // 16
    other = pl.ds(pl.multiple_of((1 - half) * 128, 128), 128)
    mine = pl.ds(pl.multiple_of(half * 128, 128), 128)
    buddy = (dp, z * 2 + 1 - c)
    edge_z = jnp.where(z == 0, 1, jnp.where(z == 1, 0, jnp.where(z == 2, 3, 2)))
    edge = (dp, edge_z * 2 + 1 - c)
    across = (dp, (3 - z) * 2 + 1 - c)
    ring = (dp + 1 - 2 * hi, (3 - z) * 2 + c)
    third = (jnp.where(hub, dp, dp + 1 - 2 * hi), (3 - z) * 2 + jnp.where(hub, 1 - c, c))
    sides = [
        (((x + 1) % 4) * 8 + y * 2 + hi, ft),
        (((x + 3) % 4) * 8 + y * 2 + hi, ft),
        (x * 8 + ((y + 1) % 4) * 2 + hi, ft),
        (x * 8 + ((y + 3) % 4) * 2 + hi, ft),
    ]

    opposite = [(((x + 2) % 4) * 8 + y * 2 + hi, ft), (x * 8 + ((y + 2) % 4) * 2 + hi, ft)]

    barrier = pltpu.get_barrier_semaphore()
    peers = [buddy, edge, third] + sides
    for peer in peers:
        pl.semaphore_signal(barrier, inc=1, device_id=peer, device_id_type=MESH)

    loads = [
        pltpu.make_async_copy(src, dst, load_sem.at[i])
        for i, (src, dst) in enumerate(
            ((p_hbm, p_ref), (e_hbm, e_ref), (w1_hbm, w1_ref), (w2_hbm, w2_ref), (c_hbm, c_ref))
        )
    ]
    for load in loads[:2]:
        load.start()

    def tell(r):
        for peer in (sides, opposite)[r]:
            pl.semaphore_signal(relay.at[r], inc=1, device_id=peer, device_id_type=MESH)

    def hear(r):
        pl.semaphore_wait(relay.at[r], (4, 2)[r])

    def tell_ring(r):
        pl.semaphore_signal(relay.at[r], inc=1, device_id=ring, device_id_type=MESH)

    def hear_ring(r):
        pl.semaphore_wait(relay.at[r], 1)

    def send(src, dst, s_sem, r_sem, device):
        return pltpu.make_async_remote_copy(
            src_ref=src, dst_ref=dst, send_sem=s_sem, recv_sem=r_sem,
            device_id=device, device_id_type=MESH,
        )

    swap = send(e_ref, e2_ref, ssem.at[0, 4], rsem.at[0, 0, 4], buddy)

    def to_buddy(q, s):
        return send(part.at[q, s, other], land_a.at[q, s], ssem.at[q, 0], rsem.at[q, s, 0], buddy)

    def to_hub(q, s):
        return send(chip.at[q, s], land_b.at[q, s], ssem.at[q, 1], rsem.at[q, s, 1], edge)

    def to_across(q, s):
        return send(pair.at[q, s], land_c.at[q, s], ssem.at[q, 1], rsem.at[q, s, 2], across)

    def to_outer(q, s):
        ref = full.at[q, s, mine]
        return send(ref, ref, ssem.at[q, 2], rsem.at[q, s, 1], edge)

    def share(q, s):
        ref = full.at[q, s, mine]
        return send(ref, ref, ssem.at[q, 3], rsem.at[q, s, 3], buddy)

    def first(q, s):
        to_buddy(q, s).wait_recv()
        chip[q, s] = (part[q, s, mine].astype(F32) + land_a[q, s].astype(F32)).astype(BF)
        to_hub(q, s).start()

    def paired(q, s):
        to_buddy(q, s).wait_recv()
        to_hub(q, s).wait_recv()
        total = part[q, s, mine].astype(F32) + land_a[q, s].astype(F32) + land_b[q, s].astype(F32)
        pair[q, s] = total.astype(BF)
        to_across(q, s).start()

    def totalled(q, s):
        to_across(q, s).wait_recv()
        full[q, s, mine] = (pair[q, s].astype(F32) + land_c[q, s].astype(F32)).astype(BF)
        to_outer(q, s).start()
        share(q, s).start()

    def shared(q, s):
        to_outer(q, s).wait_recv()
        share(q, s).start()

    loads[0].wait()
    pt_ref[...] = p_ref[...].T
    loads[1].wait()
    for load in loads[2:]:
        load.start()

    def start_samples(i, carry):
        for s in [4 * i + j for j in range(4)]:
            part[0, s] = nn(pt_ref[...], e_ref[s]).astype(BF)
        return carry

    def send_samples(s, carry):
        to_buddy(0, s).start()
        return carry

    lax.fori_loop(0, samples // 4, start_samples, 0)
    pl.semaphore_wait(barrier, len(peers))
    lax.fori_loop(0, samples, send_samples, 0)
    tell(0)
    swap.start()

    def first_samples(low, high):
        def body(s, carry):
            first(0, s)
            return carry

        lax.fori_loop(low, high, body, 0)

    @pl.when(outer)
    def _():
        first_samples(0, 6)

    hid_acc[...] = jnp.zeros_like(hid_acc)
    out_acc[...] = jnp.zeros_like(out_acc)
    proj_acc[...] = jnp.zeros_like(proj_acc)
    for ref in (*inters, *acts, *pre_cots):
        ref[...] = jnp.zeros_like(ref)
    for load in loads[2:]:
        load.wait()
    w1t_ref[...] = (w1_ref[...].T.astype(F32) * 0.5).astype(BF)
    w2h_ref[...] = (w2_ref[...].astype(F32) * 0.5).astype(BF)

    def act_cots(i, carry):
        for s in (2 * i, 2 * i + 1):
            act_cot[s] = nt(w2h_ref[...], c_ref[s])
        return carry

    lax.fori_loop(0, pairs, act_cots, 0)

    @pl.when(outer)
    def _():
        hear(0)
        tell(1)
        first_samples(6, 12)
        hear(1)
        first_samples(12, samples)

    def mlp(s, now, before):
        r = jnp.maximum(s - 1, 0)
        s = jnp.minimum(s, samples - 1)
        inter_cot = nn(w1_ref[...], pre_cots[before][...]).astype(BF)
        icot[r] = inter_cot
        inter = nt(full[0, s], e_ref[s]).astype(BF)
        hid_acc[...] += nt(inters[before][...], pre_cots[before][...])
        u = nn(w1t_ref[...], inter)
        out_acc[...] += nn(acts[before][...], c_ref[r])
        t = jnp.tanh(u)
        p = 1.0 + t
        a = u * p
        inters[now][...] = inter
        acts[now][...] = a.astype(BF)
        pre_cots[now][...] = (act_cot[s] * (p + a * (1.0 - t))).astype(BF)
        part[1, r] = nn(inter_cot, e_ref[r]).astype(BF)

    def grad_of(both):
        for s in both:
            total = tn(icot[s], full[0, s]) + nn(p_ref[...], full[1, s])
            stage[s] = (c_ref[s].astype(F32) + total).astype(BF)
            pltpu.make_async_copy(stage.at[s], eg_any.at[s], store_sem).start()

    def proj_of(own, both):
        emb = e_ref if own else e2_ref
        return sum(nt(full[1, s, mine], emb[s]) for s in both)

    def proj_some(both):
        for i in range(2):
            proj_acc[i] += proj_of(i == 0, both)

    def final(both):
        for s in both:
            share(1, s).wait_recv()
        grad_of(both)

    w_core = send(w_mine.at[:, 1 - c], w_buddy, wss.at[0], wrs.at[0], buddy)
    place = x * 4 + y
    w_xyc = []
    for d in range(1, 16):
        there = (place + d) % 16
        w_xyc.append(send(w_chip.at[there], w_xy.at[d], wss.at[1], wrs.at[1], (there * 2 + hi, ft)))
    w_xy_all = send(w_chip.at[pl.ds(0, 15)], w_xy.at[pl.ds(1, 15)], wss.at[1], wrs.at[1], buddy)
    slot = hi * 4 + z
    w_zc = [
        send(w_plane, w_z.at[slot], wss.at[2], wrs.at[2], (place * 2 + c, ((z + d) % 4) * 2 + c))
        for d in range(4)
    ]

    def w_z_some(count):
        return send(w_z.at[pl.ds(0, count)], w_z.at[pl.ds(0, count)], wss.at[2], wrs.at[2], buddy)

    w_last = send(w_all, w_all, wss.at[3], wrs.at[3], buddy)

    def w_first():
        hid = hid_acc[...].reshape(16, 2, 8, 512)
        hid = jnp.concatenate([hid[..., :256], hid[..., 256:]], axis=2)
        w_mine[..., :256] = hid.astype(BF)
        w_mine[..., 256:] = out_acc[...].reshape(16, 2, 16, 128).astype(BF)
        w_core.start()

    def w_along_xy():
        w_core.wait_recv()
        w_chip[...] = (w_mine[:, c].astype(F32) + w_buddy[...].astype(F32)).astype(BF)
        for copy in w_xyc:
            copy.start()

    def w_along_z():
        w_xy_all.wait_recv()
        total = w_chip[place].astype(F32)
        for d in range(1, 16):
            total += w_xy[d].astype(F32)
        w_plane[...] = total.astype(BF)
        for copy in w_zc[1:]:
            copy.start()

        @pl.when(c != hi)
        def _():
            w_zc[0].start()

        @pl.when(c == hi)
        def _():
            w_z[slot] = total.astype(BF)

    def w_share():
        @pl.when(c == hi)
        def _():
            w_z_some(7).wait_recv()
            total = w_z[0].astype(F32)
            for d in range(1, 8):
                total += w_z[d].astype(F32)
            w_all[...] = total
            w_last.start()

    def when(condition, act, *args):
        pl.when(condition)(lambda: act(*args))

    def within(u, lag, act, *args):
        when((u >= lag) & (u < lag + samples), act, *args, u - lag)

    def fill(u, carry):
        @pl.when(hub)
        def _():
            when(u == 0, hear, 0)
            when(u == 0, tell, 1)
            when(u == 8, hear, 1)
            paired(0, u)
            when(u >= LAG_TOTAL, totalled, 0, u - LAG_TOTAL)

        when(outer & (u >= LAG_SHARE), shared, 0, u - LAG_SHARE)
        return carry

    def middle(s, now):
        u = s + LAG_MLP

        @pl.when(hub)
        def _():
            within(u, 0, paired, 0)
            within(u, LAG_TOTAL, totalled, 0)

        @pl.when(outer)
        def _():
            within(u, LAG_SHARE, shared, 0)

        when(s < samples, lambda: share(0, s).wait_recv())
        mlp(s, now, 1 - now)
        when(s > 0, lambda: to_buddy(1, s - 1).start())

        @pl.when(outer)
        def _():
            when(s == 0, tell_ring, 2)
            when(s == 8, hear_ring, 2)
            when(s == 13, tell_ring, 3)
            within(u, LAG2_FIRST, first, 1)

        @pl.when(hub)
        def _():
            within(u, LAG2_PAIR, paired, 1)
            within(u, LAG2_TOTAL, totalled, 1)

    def middle_two(i, carry):
        middle(2 * i, 0)
        when(i < pairs, middle, 2 * i + 1, 1)
        return carry

    def drain(u, carry):
        done = samples + LAG_MLP + 1
        when(u == done, w_first)
        when(u == done, swap.wait_recv)
        when(u == done + 2, w_along_xy)

        @pl.when(outer)
        def _():
            when(u == LAG2_FIRST + samples - 1, hear_ring, 3)
            within(u, LAG2_FIRST, first, 1)
            when(u >= LAG2_SHARE, shared, 1, u - LAG2_SHARE)

        @pl.when(hub)
        def _():
            within(u, LAG2_PAIR, paired, 1)
            within(u, LAG2_TOTAL, totalled, 1)

        when(u == done + 9, w_along_z)
        s = u - LAG2_SHARE - 1

        @pl.when((s >= 0) & (s % 2 == 0))
        def _():
            proj_some([s, s + 1])
            when(s >= 2, final, [s - 2, s - 1])

        return carry

    lax.fori_loop(0, LAG_MLP, fill, 0)
    lax.fori_loop(0, pairs + 1, middle_two, 0)
    lax.fori_loop(samples + LAG_MLP + 1, samples - 2 + LAG2_SHARE, drain, 0)
    last = [samples - 2, samples - 1]

    @pl.when(outer)
    def _():
        for s in last:
            shared(1, s)

    here = p_land.at[pl.ds(dp, 1)]
    for i in range(2):
        proj = (proj_acc[i] + proj_of(i == 0, last)).reshape(16, 8, 256)
        p_mine[i] = jnp.concatenate([proj[..., :128], proj[..., 128:]], axis=1).astype(BF)
    for dh, dy, xi, i in itertools.product((1, 0), (2, 1, 3, 0), (0, 1), (0, 1)):
        there = xi * 8 + ((y + dy) % 4) * 2 + (hi + dh) % 2
        core = c if i == 0 else 1 - c
        copy = send(p_mine.at[i, pl.ds(there, 1)], here, pss, prs, (half * 16 + there, z * 2 + core))
        if dh == 0 and dy == 0 and i == 0:
            pl.when(half * 2 + xi != x)(copy.start)
        else:
            copy.start()

    @pl.when(hi_half == half)
    def _():
        p_land[dp] = p_mine[0, dp % 16]

    def p_some(count):
        return send(p_land.at[pl.ds(0, count)], p_land.at[pl.ds(0, count)], pss, prs, buddy)

    final([samples - 4, samples - 3])
    for s in last:
        share(1, s).wait_recv()
    grad_of(last)
    w_share()

    for q in range(2):
        sent = [send(chip.at[q], land_b.at[q], ssem.at[q, k], rsem.at[q, 0, 0], buddy) for k in range(4)]
        for k in (0, 1, 3):
            sent[k].wait_send()

        @pl.when(hub)
        def _():
            sent[2].wait_send()
    w_core.wait_send()
    w_xy_all.wait_send()

    @pl.when(c != hi)
    def _():
        w_z_some(4).wait_send()
        w_last.wait_recv()

    @pl.when(c == hi)
    def _():
        w_z_some(3).wait_send()
        w_last.wait_send()

    hg_ref[:, :256] = w_all[:8, :256] * mlp_scale
    hg_ref[:, 256:] = w_all[8:, :256] * mlp_scale
    og_ref[...] = w_all[:, 256:] * mlp_scale
    pltpu.make_async_copy(stage, eg_any, store_sem).wait()
    pl.when(hi_half == half)(lambda: p_some(31).wait_recv())
    pl.when(hi_half != half)(lambda: p_some(32).wait_recv())
    total = p_land[0].astype(F32)
    for d in range(1, 32):
        total += p_land[d].astype(F32)
    pg_ref[:, :128] = total[:8] * proj_scale
    pg_ref[:, 128:] = total[8:] * proj_scale
    swap.wait_send()
    pl.when(hi_half == half)(lambda: p_some(31).wait_send())
    pl.when(hi_half != half)(lambda: p_some(32).wait_send())


def finish(eg_in, pg_in, hg_in, og_in, eg_out, pg_out, hg_out, og_out, eg, pg, hg, og, in_sem, out_sem):
    parts = in_sem.shape[0] - 3
    rows = eg.shape[0] // parts
    moves = [(pg_in, pg, pg_out), (hg_in, hg, hg_out), (og_in, og, og_out)]
    for i in range(parts):
        some = pl.ds(i * rows, rows)
        moves.append((eg_in.at[some], eg.at[some], eg_out.at[some]))
    loads = [pltpu.make_async_copy(m[0], m[1], in_sem.at[i]) for i, m in enumerate(moves)]
    stores = [pltpu.make_async_copy(m[1], m[2], out_sem.at[i]) for i, m in enumerate(moves)]
    for load in loads:
        load.start()
    for load, store in zip(loads, stores):
        load.wait()
        store.start()
    for store in stores:
        store.wait()


def local(embeds, proj_weight, hidden_weight, out_weight, cotangent):
    n, f, d = embeds.shape
    k = proj_weight.shape[1]
    h = hidden_weight.shape[1]
    dp_count = lax.axis_size("dp")
    mlp_scale = 4.0 / (n * dp_count)
    proj_scale = 1.0 / (n * dp_count * math.sqrt(d))
    vmem = pltpu.VMEM
    dma = pltpu.SemaphoreType.DMA
    hbm = pl.BlockSpec(memory_space=pltpu.HBM)
    anywhere = pl.BlockSpec(memory_space=pl.ANY)
    inside = pl.BlockSpec(memory_space=pltpu.VMEM)
    shapes = (
        jax.ShapeDtypeStruct((n, f, d), BF),
        jax.ShapeDtypeStruct((8, f), F32),
        jax.ShapeDtypeStruct((8, h), F32),
        jax.ShapeDtypeStruct((16, d), F32),
    )
    results = pl.pallas_call(
        functools.partial(kernel, n, proj_scale, mlp_scale),
        out_shape=shapes,
        in_specs=[hbm] * 5,
        out_specs=(anywhere, inside, inside, inside),
        scratch_shapes=[
            vmem((n, f, d), BF), vmem((f, k), BF), vmem((k, h), BF), vmem((h, d), BF), vmem((n, f, d), BF),
            vmem((k, f), BF), vmem((h, k), BF), vmem((h, d), BF),
            vmem((2, n, k, d), BF),
            vmem((2, n, k // 2, d), BF),
            vmem((2, n, k // 2, d), BF),
            vmem((2, n, k // 2, d), BF),
            vmem((2, n, k // 2, d), BF),
            vmem((2, n, k // 2, d), BF),
            vmem((2, n, k, d), BF),
            vmem((n, h, f), F32),
            vmem((n, k, f), BF),
            [vmem((k, f), BF)] * 2, [vmem((h, f), BF)] * 2, [vmem((h, f), BF)] * 2,
            vmem((n, f, d), BF),
            vmem((k, h), F32), vmem((h, d), F32), vmem((2, k // 2, f), F32),
            vmem((16, 2, 16, 384), BF), vmem((16, 16, 384), BF), vmem((16, 16, 384), BF),
            vmem((16, 16, 384), BF), vmem((16, 384), BF), vmem((8, 16, 384), BF), vmem((16, 384), F32),
            vmem((2, 16, 16, 128), BF), vmem((32, 16, 128), BF), vmem((n, f, d), BF),
            dma((5,)), dma, dma((2, 5)), dma((2, n, 5)),
            dma((4,)), dma((4,)), dma, dma, pltpu.SemaphoreType.REGULAR((4,)),
        ],
        compiler_params=pltpu.CompilerParams(
            collective_id=0, has_side_effects=True, vmem_limit_bytes=int(53.9 * 1024) * 1024
        ),
    )(embeds, proj_weight, hidden_weight, out_weight, cotangent)
    grad, proj, hid, out = pl.pallas_call(
        finish,
        out_shape=shapes,
        in_specs=[hbm] * 4,
        out_specs=(hbm,) * 4,
        scratch_shapes=[vmem(v.shape, v.dtype) for v in shapes] + [dma((7,)), dma((7,))],
        compiler_params=pltpu.CompilerParams(vmem_limit_bytes=int(53.9 * 1024) * 1024),
    )(*results)
    return grad, proj.T, hid, out


def solution(mesh):
    placed = (P("dp", "feat", None), P("feat", None), P(), P(), P("dp", "feat", None))
    return jax.shard_map(
        local,
        mesh=mesh,
        in_specs=placed,
        out_specs=(P("dp", "feat", None), P("feat", "dp"), P("dp", None), P("dp", None)),
        check_vma=False,
    )
```

```python
import functools
import itertools
import math

import jax
import jax.numpy as jnp
from jax import lax
from jax.experimental import pallas as pl
from jax.experimental.pallas import tpu as pltpu
from jax.sharding import PartitionSpec as P

MESH = pl.DeviceIdType.MESH
BF = jnp.bfloat16
F32 = jnp.float32

LAG_TOTAL = 5
LAG_SHARE = 10
LAG_MLP = 12
LAG2_FIRST = 14
LAG2_PAIR = 19
LAG2_TOTAL = 24
LAG2_SHARE = 29


def nn(a, b):
    return lax.dot_general(a, b, (((1,), (0,)), ((), ())), preferred_element_type=F32)


def nt(a, b):
    return lax.dot_general(a, b, (((1,), (1,)), ((), ())), preferred_element_type=F32)


def tn(a, b):
    return lax.dot_general(a, b, (((0,), (0,)), ((), ())), preferred_element_type=F32)


def kernel(
    samples, proj_scale, mlp_scale, e_hbm, p_hbm, w1_hbm, w2_hbm, c_hbm,
    eg_ref, pg_ref, hg_ref, og_ref,
    e_ref, p_ref, w1_ref, w2_ref, c_ref, pt_ref, w1t_ref, w2h_ref,
    part, land_a, chip, land_b, pair, land_c, full,
    act_cot, icot, inters, acts, pre_cots, hid_acc, out_acc, proj_acc,
    w_mine, w_buddy, w_chip, w_xy, w_plane, w_z, w_all,
    p_mine, p_land,
    e2_ref, load_sem, ssem, rsem, wss, wrs, pss, prs, relay,
):
    pairs = samples // 2
    dp, ft = lax.axis_index("dp"), lax.axis_index("feat")
    x, y, hi = dp // 8, (dp // 2) % 4, dp % 2
    z, c = ft // 2, ft % 2
    hub = (z == 1) | (z == 2)
    outer = (z == 0) | (z == 3)
    half = (c + z) % 2
    hi_half = dp // 16
    other = pl.ds(pl.multiple_of((1 - half) * 128, 128), 128)
    mine = pl.ds(pl.multiple_of(half * 128, 128), 128)
    buddy = (dp, z * 2 + 1 - c)
    edge_z = jnp.where(z == 0, 1, jnp.where(z == 1, 0, jnp.where(z == 2, 3, 2)))
    edge = (dp, edge_z * 2 + 1 - c)
    across = (dp, (3 - z) * 2 + 1 - c)
    ring = (dp + 1 - 2 * hi, (3 - z) * 2 + c)
    third = (jnp.where(hub, dp, dp + 1 - 2 * hi), (3 - z) * 2 + jnp.where(hub, 1 - c, c))
    sides = [
        (((x + 1) % 4) * 8 + y * 2 + hi, ft),
        (((x + 3) % 4) * 8 + y * 2 + hi, ft),
        (x * 8 + ((y + 1) % 4) * 2 + hi, ft),
        (x * 8 + ((y + 3) % 4) * 2 + hi, ft),
    ]

    opposite = [(((x + 2) % 4) * 8 + y * 2 + hi, ft), (x * 8 + ((y + 2) % 4) * 2 + hi, ft)]

    barrier = pltpu.get_barrier_semaphore()
    peers = [buddy, edge, third] + sides
    for peer in peers:
        pl.semaphore_signal(barrier, inc=1, device_id=peer, device_id_type=MESH)

    loads = [
        pltpu.make_async_copy(src, dst, load_sem.at[i])
        for i, (src, dst) in enumerate(
            ((p_hbm, p_ref), (e_hbm, e_ref), (w1_hbm, w1_ref), (w2_hbm, w2_ref), (c_hbm, c_ref))
        )
    ]
    for load in loads[:2]:
        load.start()

    def tell(r):
        for peer in (sides, opposite)[r]:
            pl.semaphore_signal(relay.at[r], inc=1, device_id=peer, device_id_type=MESH)

    def hear(r):
        pl.semaphore_wait(relay.at[r], (4, 2)[r])

    def tell_ring(r):
        pl.semaphore_signal(relay.at[r], inc=1, device_id=ring, device_id_type=MESH)

    def hear_ring(r):
        pl.semaphore_wait(relay.at[r], 1)

    def send(src, dst, s_sem, r_sem, device):
        return pltpu.make_async_remote_copy(
            src_ref=src, dst_ref=dst, send_sem=s_sem, recv_sem=r_sem,
            device_id=device, device_id_type=MESH,
        )

    swap = send(e_ref, e2_ref, ssem.at[0, 4], rsem.at[0, 0, 4], buddy)

    def to_buddy(q, s):
        return send(part.at[q, s, other], land_a.at[q, s], ssem.at[q, 0], rsem.at[q, s, 0], buddy)

    def to_hub(q, s):
        return send(chip.at[q, s], land_b.at[q, s], ssem.at[q, 1], rsem.at[q, s, 1], edge)

    def to_across(q, s):
        return send(pair.at[q, s], land_c.at[q, s], ssem.at[q, 1], rsem.at[q, s, 2], across)

    def to_outer(q, s):
        ref = full.at[q, s, mine]
        return send(ref, ref, ssem.at[q, 2], rsem.at[q, s, 1], edge)

    def share(q, s):
        ref = full.at[q, s, mine]
        return send(ref, ref, ssem.at[q, 3], rsem.at[q, s, 3], buddy)

    def first(q, s):
        to_buddy(q, s).wait_recv()
        chip[q, s] = (part[q, s, mine].astype(F32) + land_a[q, s].astype(F32)).astype(BF)
        to_hub(q, s).start()

    def paired(q, s):
        to_buddy(q, s).wait_recv()
        to_hub(q, s).wait_recv()
        total = part[q, s, mine].astype(F32) + land_a[q, s].astype(F32) + land_b[q, s].astype(F32)
        pair[q, s] = total.astype(BF)
        to_across(q, s).start()

    def totalled(q, s):
        to_across(q, s).wait_recv()
        full[q, s, mine] = (pair[q, s].astype(F32) + land_c[q, s].astype(F32)).astype(BF)
        to_outer(q, s).start()
        share(q, s).start()

    def shared(q, s):
        to_outer(q, s).wait_recv()
        share(q, s).start()

    loads[0].wait()
    pt_ref[...] = p_ref[...].T
    loads[1].wait()
    for load in loads[2:]:
        load.start()

    def start_samples(i, carry):
        for s in [4 * i + j for j in range(4)]:
            part[0, s] = nn(pt_ref[...], e_ref[s]).astype(BF)
        return carry

    def send_samples(s, carry):
        to_buddy(0, s).start()
        return carry

    lax.fori_loop(0, samples // 4, start_samples, 0)
    pl.semaphore_wait(barrier, len(peers))
    lax.fori_loop(0, samples, send_samples, 0)
    tell(0)
    swap.start()

    def first_samples(low, high):
        def body(s, carry):
            first(0, s)
            return carry

        lax.fori_loop(low, high, body, 0)

    @pl.when(outer)
    def _():
        first_samples(0, 6)

    hid_acc[...] = jnp.zeros_like(hid_acc)
    out_acc[...] = jnp.zeros_like(out_acc)
    proj_acc[...] = jnp.zeros_like(proj_acc)
    for ref in (inters, acts, pre_cots):
        ref[...] = jnp.zeros_like(ref)
    for load in loads[2:]:
        load.wait()
    w1t_ref[...] = (w1_ref[...].T.astype(F32) * 0.5).astype(BF)
    w2h_ref[...] = (w2_ref[...].astype(F32) * 0.5).astype(BF)

    def act_cots(i, carry):
        for s in (2 * i, 2 * i + 1):
            act_cot[s] = nt(w2h_ref[...], c_ref[s])
        return carry

    lax.fori_loop(0, pairs, act_cots, 0)

    @pl.when(outer)
    def _():
        hear(0)
        tell(1)
        first_samples(6, 12)
        hear(1)
        first_samples(12, samples)

    def mlp(s, now, before):
        r = jnp.maximum(s - 1, 0)
        s = jnp.minimum(s, samples - 1)
        inter_cot = nn(w1_ref[...], pre_cots[before]).astype(BF)
        icot[r] = inter_cot
        inter = nt(full[0, s], e_ref[s]).astype(BF)
        hid_acc[...] += nt(inters[before], pre_cots[before])
        u = nn(w1t_ref[...], inter)
        out_acc[...] += nn(acts[before], c_ref[r])
        t = jnp.tanh(u)
        p = 1.0 + t
        a = u * p
        inters[now] = inter
        acts[now] = a.astype(BF)
        pre_cots[now] = (act_cot[s] * (p + a * (1.0 - t))).astype(BF)
        part[1, r] = nn(inter_cot, e_ref[r]).astype(BF)

    def grad_of(both):
        for s in both:
            total = tn(icot[s], full[0, s]) + nn(p_ref[...], full[1, s])
            eg_ref[s] = (c_ref[s].astype(F32) + total).astype(BF)

    def proj_of(own, both):
        emb = e_ref if own else e2_ref
        return sum(nt(full[1, s, mine], emb[s]) for s in both)

    def proj_some(both):
        for i in range(2):
            proj_acc[i] += proj_of(i == 0, both)

    def final(both):
        for s in both:
            share(1, s).wait_recv()
        grad_of(both)

    w_core = send(w_mine.at[:, 1 - c], w_buddy, wss.at[0], wrs.at[0], buddy)
    place = x * 4 + y
    w_xyc = []
    for d in range(1, 16):
        there = (place + d) % 16
        w_xyc.append(send(w_chip.at[there], w_xy.at[d], wss.at[1], wrs.at[1], (there * 2 + hi, ft)))
    w_xy_all = send(w_chip.at[pl.ds(0, 15)], w_xy.at[pl.ds(1, 15)], wss.at[1], wrs.at[1], buddy)
    slot = hi * 4 + z
    w_zc = [
        send(w_plane, w_z.at[slot], wss.at[2], wrs.at[2], (place * 2 + c, ((z + d) % 4) * 2 + c))
        for d in range(4)
    ]

    def w_z_some(count):
        return send(w_z.at[pl.ds(0, count)], w_z.at[pl.ds(0, count)], wss.at[2], wrs.at[2], buddy)

    w_last = send(w_all, w_all, wss.at[3], wrs.at[3], buddy)

    def w_first():
        hid = hid_acc[...].reshape(16, 2, 8, 512)
        hid = jnp.concatenate([hid[..., :256], hid[..., 256:]], axis=2)
        w_mine[..., :256] = hid.astype(BF)
        w_mine[..., 256:] = out_acc[...].reshape(16, 2, 16, 128).astype(BF)
        w_core.start()

    def w_along_xy():
        w_core.wait_recv()
        w_chip[...] = (w_mine[:, c].astype(F32) + w_buddy[...].astype(F32)).astype(BF)
        for copy in w_xyc:
            copy.start()

    def w_along_z():
        w_xy_all.wait_recv()
        total = w_chip[place].astype(F32)
        for d in range(1, 16):
            total += w_xy[d].astype(F32)
        w_plane[...] = total.astype(BF)
        for copy in w_zc[1:]:
            copy.start()

        @pl.when(c != hi)
        def _():
            w_zc[0].start()

        @pl.when(c == hi)
        def _():
            w_z[slot] = total.astype(BF)

    def w_share():
        @pl.when(c == hi)
        def _():
            w_z_some(7).wait_recv()
            total = w_z[0].astype(F32)
            for d in range(1, 8):
                total += w_z[d].astype(F32)
            w_all[...] = total
            w_last.start()

    def when(condition, act, *args):
        pl.when(condition)(lambda: act(*args))

    def within(u, lag, act, *args):
        when((u >= lag) & (u < lag + samples), act, *args, u - lag)

    def fill(u, carry):
        @pl.when(hub)
        def _():
            when(u == 0, hear, 0)
            when(u == 0, tell, 1)
            when(u == 8, hear, 1)
            paired(0, u)
            when(u >= LAG_TOTAL, totalled, 0, u - LAG_TOTAL)

        when(outer & (u >= LAG_SHARE), shared, 0, u - LAG_SHARE)
        return carry

    def middle(s, carry):
        u = s + LAG_MLP
        now = s % 2

        @pl.when(hub)
        def _():
            within(u, 0, paired, 0)
            within(u, LAG_TOTAL, totalled, 0)

        @pl.when(outer)
        def _():
            within(u, LAG_SHARE, shared, 0)

        when(s < samples, lambda: share(0, s).wait_recv())
        mlp(s, now, 1 - now)
        when(s > 0, lambda: to_buddy(1, s - 1).start())

        @pl.when(outer)
        def _():
            when(s == 0, tell_ring, 2)
            when(s == 8, hear_ring, 2)
            when(s == 13, tell_ring, 3)
            within(u, LAG2_FIRST, first, 1)

        @pl.when(hub)
        def _():
            within(u, LAG2_PAIR, paired, 1)
            within(u, LAG2_TOTAL, totalled, 1)

        return carry

    def drain(u, carry):
        done = samples + LAG_MLP + 1
        when(u == done, w_first)
        when(u == done, swap.wait_recv)
        when(u == done + 2, w_along_xy)

        @pl.when(outer)
        def _():
            when(u == LAG2_FIRST + samples - 1, hear_ring, 3)
            within(u, LAG2_FIRST, first, 1)
            when(u >= LAG2_SHARE, shared, 1, u - LAG2_SHARE)

        @pl.when(hub)
        def _():
            within(u, LAG2_PAIR, paired, 1)
            within(u, LAG2_TOTAL, totalled, 1)

        when(u == done + 9, w_along_z)
        s = u - LAG2_SHARE - 1

        @pl.when((s >= 0) & (s % 2 == 0))
        def _():
            proj_some([s, s + 1])
            when(s >= 2, final, [s - 2, s - 1])

        return carry

    lax.fori_loop(0, LAG_MLP, fill, 0)
    lax.fori_loop(0, samples + 1, middle, 0)
    lax.fori_loop(samples + LAG_MLP + 1, samples - 2 + LAG2_SHARE, drain, 0)
    last = [samples - 2, samples - 1]

    @pl.when(outer)
    def _():
        for s in last:
            shared(1, s)

    here = p_land.at[pl.ds(dp, 1)]
    for i in range(2):
        proj = (proj_acc[i] + proj_of(i == 0, last)).reshape(16, 8, 256)
        p_mine[i] = jnp.concatenate([proj[..., :128], proj[..., 128:]], axis=1).astype(BF)
    for dh, dy, xi, i in itertools.product((1, 0), (2, 1, 3, 0), (0, 1), (0, 1)):
        there = xi * 8 + ((y + dy) % 4) * 2 + (hi + dh) % 2
        core = c if i == 0 else 1 - c
        copy = send(p_mine.at[i, pl.ds(there, 1)], here, pss, prs, (half * 16 + there, z * 2 + core))
        if dh == 0 and dy == 0 and i == 0:
            pl.when(half * 2 + xi != x)(copy.start)
        else:
            copy.start()

    @pl.when(hi_half == half)
    def _():
        p_land[dp] = p_mine[0, dp % 16]

    def p_some(count):
        return send(p_land.at[pl.ds(0, count)], p_land.at[pl.ds(0, count)], pss, prs, buddy)

    final([samples - 4, samples - 3])
    for s in last:
        share(1, s).wait_recv()
    grad_of(last)
    w_share()

    for q in range(2):
        sent = [send(chip.at[q], land_b.at[q], ssem.at[q, k], rsem.at[q, 0, 0], buddy) for k in range(4)]
        for k in (0, 1, 3):
            sent[k].wait_send()

        @pl.when(hub)
        def _():
            sent[2].wait_send()
    w_core.wait_send()
    w_xy_all.wait_send()

    @pl.when(c != hi)
    def _():
        w_z_some(4).wait_send()
        w_last.wait_recv()

    @pl.when(c == hi)
    def _():
        w_z_some(3).wait_send()
        w_last.wait_send()

    hg_ref[:, :256] = w_all[:8, :256] * mlp_scale
    hg_ref[:, 256:] = w_all[8:, :256] * mlp_scale
    og_ref[...] = w_all[:, 256:] * mlp_scale
    pl.when(hi_half == half)(lambda: p_some(31).wait_recv())
    pl.when(hi_half != half)(lambda: p_some(32).wait_recv())
    total = p_land[0].astype(F32)
    for d in range(1, 32):
        total += p_land[d].astype(F32)
    pg_ref[:, :128] = total[:8] * proj_scale
    pg_ref[:, 128:] = total[8:] * proj_scale
    swap.wait_send()
    pl.when(hi_half == half)(lambda: p_some(31).wait_send())
    pl.when(hi_half != half)(lambda: p_some(32).wait_send())


def finish(*refs):
    count = (len(refs) - 1) // 2
    copies = [pltpu.make_async_copy(refs[i], refs[count + i], refs[-1].at[i]) for i in range(count)]
    for copy in copies:
        copy.start()
    for copy in copies:
        copy.wait()


def local(embeds, proj_weight, hidden_weight, out_weight, cotangent):
    n, f, d = embeds.shape
    k = proj_weight.shape[1]
    h = hidden_weight.shape[1]
    dp_count = lax.axis_size("dp")
    mlp_scale = 4.0 / (n * dp_count)
    proj_scale = 1.0 / (n * dp_count * math.sqrt(d))
    vmem = pltpu.VMEM
    dma = pltpu.SemaphoreType.DMA
    hbm = pl.BlockSpec(memory_space=pltpu.HBM)
    anywhere = pl.BlockSpec(memory_space=pl.ANY)
    inside = pl.BlockSpec(memory_space=pltpu.VMEM)
    shapes = (
        jax.ShapeDtypeStruct((n, f, d), BF),
        jax.ShapeDtypeStruct((8, f), F32),
        jax.ShapeDtypeStruct((8, h), F32),
        jax.ShapeDtypeStruct((16, d), F32),
    )
    results = pl.pallas_call(
        functools.partial(kernel, n, proj_scale, mlp_scale),
        out_shape=tuple(vmem(v.shape, v.dtype) for v in shapes),
        in_specs=[hbm] * 5,
        out_specs=(inside,) * 4,
        scratch_shapes=[
            vmem((n, f, d), BF), vmem((f, k), BF), vmem((k, h), BF), vmem((h, d), BF), vmem((n, f, d), BF),
            vmem((k, f), BF), vmem((h, k), BF), vmem((h, d), BF),
            vmem((2, n, k, d), BF),
            vmem((2, n, k // 2, d), BF),
            vmem((2, n, k // 2, d), BF),
            vmem((2, n, k // 2, d), BF),
            vmem((2, n, k // 2, d), BF),
            vmem((2, n, k // 2, d), BF),
            vmem((2, n, k, d), BF),
            vmem((n, h, f), F32),
            vmem((n, k, f), BF),
            vmem((2, k, f), BF), vmem((2, h, f), BF), vmem((2, h, f), BF),
            vmem((k, h), F32), vmem((h, d), F32), vmem((2, k // 2, f), F32),
            vmem((16, 2, 16, 384), BF), vmem((16, 16, 384), BF), vmem((16, 16, 384), BF),
            vmem((16, 16, 384), BF), vmem((16, 384), BF), vmem((8, 16, 384), BF), vmem((16, 384), F32),
            vmem((2, 16, 16, 128), BF), vmem((32, 16, 128), BF), vmem((n, f, d), BF),
            dma((5,)), dma((2, 5)), dma((2, n, 5)),
            dma((4,)), dma((4,)), dma, dma, pltpu.SemaphoreType.REGULAR((4,)),
        ],
        compiler_params=pltpu.CompilerParams(
            collective_id=0, has_side_effects=True, vmem_limit_bytes=48 * 1024 * 1024
        ),
    )(*[pltpu.with_memory_space_constraint(v, pltpu.HBM) for v in (embeds, proj_weight, hidden_weight, out_weight, cotangent)])
    grad, proj, hid, out = pl.pallas_call(
        finish,
        out_shape=shapes,
        in_specs=[inside] * 4,
        out_specs=(hbm,) * 4,
        scratch_shapes=[dma((4,))],
        compiler_params=pltpu.CompilerParams(vmem_limit_bytes=48 * 1024 * 1024),
    )(*results)
    return grad, proj.T, hid, out


def solution(mesh):
    placed = (P("dp", "feat", None), P("feat", None), P(), P(), P("dp", "feat", None))
    return jax.shard_map(
        local,
        mesh=mesh,
        in_specs=placed,
        out_specs=(P("dp", "feat", None), P("feat", "dp"), P("dp", None), P("dp", None)),
        check_vma=False,
    )
```

```python
import functools
import itertools
import math

import jax
import jax.numpy as jnp
from jax import lax
from jax.experimental import pallas as pl
from jax.experimental.pallas import tpu as pltpu
from jax.sharding import PartitionSpec as P

MESH = pl.DeviceIdType.MESH
BF = jnp.bfloat16
F32 = jnp.float32

LAG_TOTAL = 4
LAG_SHARE = 8
LAG_MLP = 10
LAG_MLP_HUB = 6
LAG2_FIRST = 12
LAG2_PAIR = 17
LAG2_TOTAL = 21
LAG2_SHARE = 27


def nn(a, b):
    return lax.dot_general(a, b, (((1,), (0,)), ((), ())), preferred_element_type=F32)


def nt(a, b):
    return lax.dot_general(a, b, (((1,), (1,)), ((), ())), preferred_element_type=F32)


def tn(a, b):
    return lax.dot_general(a, b, (((0,), (0,)), ((), ())), preferred_element_type=F32)


def kernel(
    samples, proj_scale, mlp_scale, e_hbm, p_hbm, w1_hbm, w2_hbm, c_hbm,
    eg_ref, pg_ref, hg_ref, og_ref,
    e_ref, p_ref, w1_ref, w2_ref, c_ref, pt_ref, w1t_ref, w2h_ref,
    part, land_a, chip, land_b, pair, land_c, full,
    act_cot, icot, inters, acts, pre_cots, hid_acc, out_acc, proj_acc,
    w_mine, w_buddy, w_chip, w_xy, w_plane, w_z, w_all,
    p_mine, p_land,
    e2_ref, load_sem, ssem, rsem, wss, wrs, pss, prs, relay,
):
    pairs = samples // 2
    dp, ft = lax.axis_index("dp"), lax.axis_index("feat")
    x, y, hi = dp // 8, (dp // 2) % 4, dp % 2
    z, c = ft // 2, ft % 2
    hub = (z == 1) | (z == 2)
    outer = (z == 0) | (z == 3)
    half = (c + z) % 2
    hi_half = dp // 16
    other = pl.ds(pl.multiple_of((1 - half) * 128, 128), 128)
    mine = pl.ds(pl.multiple_of(half * 128, 128), 128)
    buddy = (dp, z * 2 + 1 - c)
    edge_z = jnp.where(z == 0, 1, jnp.where(z == 1, 0, jnp.where(z == 2, 3, 2)))
    edge = (dp, edge_z * 2 + 1 - c)
    across = (dp, (3 - z) * 2 + 1 - c)
    ring = (dp + 1 - 2 * hi, (3 - z) * 2 + c)
    third = (jnp.where(hub, dp, dp + 1 - 2 * hi), (3 - z) * 2 + jnp.where(hub, 1 - c, c))
    sides = [
        (((x + 1) % 4) * 8 + y * 2 + hi, ft),
        (((x + 3) % 4) * 8 + y * 2 + hi, ft),
        (x * 8 + ((y + 1) % 4) * 2 + hi, ft),
        (x * 8 + ((y + 3) % 4) * 2 + hi, ft),
    ]

    opposite = [(((x + 2) % 4) * 8 + y * 2 + hi, ft), (x * 8 + ((y + 2) % 4) * 2 + hi, ft)]

    barrier = pltpu.get_barrier_semaphore()
    peers = [buddy, edge, third] + sides
    for peer in peers:
        pl.semaphore_signal(barrier, inc=1, device_id=peer, device_id_type=MESH)

    loads = [
        pltpu.make_async_copy(src, dst, load_sem.at[i])
        for i, (src, dst) in enumerate(
            ((p_hbm, p_ref), (e_hbm, e_ref), (w1_hbm, w1_ref), (w2_hbm, w2_ref), (c_hbm, c_ref))
        )
    ]
    for load in loads[:2]:
        load.start()

    def tell(r):
        for peer in (sides, opposite)[r]:
            pl.semaphore_signal(relay.at[r], inc=1, device_id=peer, device_id_type=MESH)

    def hear(r):
        pl.semaphore_wait(relay.at[r], (4, 2)[r])

    def tell_ring(r):
        pl.semaphore_signal(relay.at[r], inc=1, device_id=ring, device_id_type=MESH)

    def hear_ring(r):
        pl.semaphore_wait(relay.at[r], 1)

    def send(src, dst, s_sem, r_sem, device):
        return pltpu.make_async_remote_copy(
            src_ref=src, dst_ref=dst, send_sem=s_sem, recv_sem=r_sem,
            device_id=device, device_id_type=MESH,
        )

    swap = send(e_ref, e2_ref, ssem.at[0, 4], rsem.at[0, 0, 4], buddy)

    def to_buddy(q, s):
        return send(part.at[q, s, other], land_a.at[q, s], ssem.at[q, 0], rsem.at[q, s, 0], buddy)

    def to_hub(q, s):
        return send(chip.at[q, s], land_b.at[q, s], ssem.at[q, 1], rsem.at[q, s, 1], edge)

    def to_across(q, s):
        return send(pair.at[q, s], land_c.at[q, s], ssem.at[q, 1], rsem.at[q, s, 2], across)

    def to_outer(q, s):
        ref = full.at[q, s, mine]
        return send(ref, ref, ssem.at[q, 2], rsem.at[q, s, 1], edge)

    def share(q, s):
        ref = full.at[q, s, mine]
        return send(ref, ref, ssem.at[q, 3], rsem.at[q, s, 3], buddy)

    def first(q, s):
        to_buddy(q, s).wait_recv()
        chip[q, s] = (part[q, s, mine].astype(F32) + land_a[q, s].astype(F32)).astype(BF)
        to_hub(q, s).start()

    def paired(q, s):
        to_buddy(q, s).wait_recv()
        to_hub(q, s).wait_recv()
        total = part[q, s, mine].astype(F32) + land_a[q, s].astype(F32) + land_b[q, s].astype(F32)
        pair[q, s] = total.astype(BF)
        to_across(q, s).start()

    def totalled(q, s):
        to_across(q, s).wait_recv()
        full[q, s, mine] = (pair[q, s].astype(F32) + land_c[q, s].astype(F32)).astype(BF)
        to_outer(q, s).start()
        share(q, s).start()

    def shared(q, s):
        to_outer(q, s).wait_recv()
        share(q, s).start()

    loads[0].wait()
    pt_ref[...] = p_ref[...].T
    loads[1].wait()
    for load in loads[2:]:
        load.start()

    def start_samples(i, carry):
        for s in [4 * i + j for j in range(4)]:
            part[0, s] = nn(pt_ref[...], e_ref[s]).astype(BF)
        return carry

    def send_samples(s, carry):
        to_buddy(0, s).start()
        return carry

    lax.fori_loop(0, samples // 4, start_samples, 0)
    pl.semaphore_wait(barrier, len(peers))
    lax.fori_loop(0, samples, send_samples, 0)
    tell(0)
    swap.start()

    def first_samples(low, high):
        def body(s, carry):
            first(0, s)
            return carry

        lax.fori_loop(low, high, body, 0)

    @pl.when(outer)
    def _():
        first_samples(0, 6)

    hid_acc[...] = jnp.zeros_like(hid_acc)
    out_acc[...] = jnp.zeros_like(out_acc)
    proj_acc[...] = jnp.zeros_like(proj_acc)
    for ref in (inters, acts, pre_cots):
        ref[...] = jnp.zeros_like(ref)
    for load in loads[2:]:
        load.wait()
    w1t_ref[...] = (w1_ref[...].T.astype(F32) * 0.5).astype(BF)
    w2h_ref[...] = (w2_ref[...].astype(F32) * 0.5).astype(BF)

    def act_cots(i, carry):
        for s in (2 * i, 2 * i + 1):
            act_cot[s] = nt(w2h_ref[...], c_ref[s])
        return carry

    lax.fori_loop(0, pairs, act_cots, 0)

    @pl.when(outer)
    def _():
        hear(0)
        tell(1)
        first_samples(6, 12)
        hear(1)
        first_samples(12, samples)

    def mlp(s, now, before):
        r = jnp.maximum(s - 1, 0)
        s = jnp.minimum(s, samples - 1)
        inter_cot = nn(w1_ref[...], pre_cots[before]).astype(BF)
        icot[r] = inter_cot
        inter = nt(full[0, s], e_ref[s]).astype(BF)
        hid_acc[...] += nt(inters[before], pre_cots[before])
        u = nn(w1t_ref[...], inter)
        out_acc[...] += nn(acts[before], c_ref[r])
        t = jnp.tanh(u)
        p = 1.0 + t
        a = u * p
        inters[now] = inter
        acts[now] = a.astype(BF)
        pre_cots[now] = (act_cot[s] * (p + a * (1.0 - t))).astype(BF)
        part[1, r] = nn(inter_cot, e_ref[r]).astype(BF)

    def grad_of(both):
        for s in both:
            total = tn(icot[s], full[0, s]) + nn(p_ref[...], full[1, s])
            eg_ref[s] = (c_ref[s].astype(F32) + total).astype(BF)

    def proj_of(own, both):
        emb = e_ref if own else e2_ref
        return sum(nt(full[1, s, mine], emb[s]) for s in both)

    def proj_some(both):
        for i in range(2):
            proj_acc[i] += proj_of(i == 0, both)

    def final(both):
        for s in both:
            share(1, s).wait_recv()
        grad_of(both)

    w_core = send(w_mine.at[:, 1 - c], w_buddy, wss.at[0], wrs.at[0], buddy)
    place = x * 4 + y
    w_xyc = []
    for d in range(1, 16):
        there = (place + d) % 16
        w_xyc.append(send(w_chip.at[there], w_xy.at[d], wss.at[1], wrs.at[1], (there * 2 + hi, ft)))
    w_xy_all = send(w_chip.at[pl.ds(0, 15)], w_xy.at[pl.ds(1, 15)], wss.at[1], wrs.at[1], buddy)
    slot = hi * 4 + z
    w_zc = [
        send(w_plane, w_z.at[slot], wss.at[2], wrs.at[2], (place * 2 + c, ((z + d) % 4) * 2 + c))
        for d in range(4)
    ]

    def w_z_some(count):
        return send(w_z.at[pl.ds(0, count)], w_z.at[pl.ds(0, count)], wss.at[2], wrs.at[2], buddy)

    w_last = send(w_all, w_all, wss.at[3], wrs.at[3], buddy)

    def w_first():
        hid = hid_acc[...].reshape(16, 2, 8, 512)
        hid = jnp.concatenate([hid[..., :256], hid[..., 256:]], axis=2)
        w_mine[..., :256] = hid.astype(BF)
        w_mine[..., 256:] = out_acc[...].reshape(16, 2, 16, 128).astype(BF)
        w_core.start()

    def w_along_xy():
        w_core.wait_recv()
        w_chip[...] = (w_mine[:, c].astype(F32) + w_buddy[...].astype(F32)).astype(BF)
        for copy in w_xyc:
            copy.start()

    def w_along_z():
        w_xy_all.wait_recv()
        total = w_chip[place].astype(F32)
        for d in range(1, 16):
            total += w_xy[d].astype(F32)
        w_plane[...] = total.astype(BF)
        for copy in w_zc[1:]:
            copy.start()

        @pl.when(c != hi)
        def _():
            w_zc[0].start()

        @pl.when(c == hi)
        def _():
            w_z[slot] = total.astype(BF)

    def w_share():
        @pl.when(c == hi)
        def _():
            w_z_some(7).wait_recv()
            total = w_z[0].astype(F32)
            for d in range(1, 8):
                total += w_z[d].astype(F32)
            w_all[...] = total
            w_last.start()

    def when(condition, act, *args):
        pl.when(condition)(lambda: act(*args))

    def within(u, lag, act, *args):
        when((u >= lag) & (u < lag + samples), act, *args, u - lag)

    lag_mlp = jnp.where(hub, LAG_MLP_HUB, LAG_MLP)

    def fill(u, carry):
        @pl.when(hub)
        def _():
            when(u == 0, hear, 0)
            when(u == 0, tell, 1)
            paired(0, u)
            when(u >= LAG_TOTAL, totalled, 0, u - LAG_TOTAL)

        when(outer & (u >= LAG_SHARE), shared, 0, u - LAG_SHARE)
        return carry

    def middle(s, carry):
        u = s + lag_mlp
        now = s % 2

        @pl.when(hub)
        def _():
            when(u == 8, hear, 1)
            within(u, 0, paired, 0)
            within(u, LAG_TOTAL, totalled, 0)

        @pl.when(outer)
        def _():
            within(u, LAG_SHARE, shared, 0)

        when(s < samples, lambda: share(0, s).wait_recv())
        mlp(s, now, 1 - now)
        when(s > 0, lambda: to_buddy(1, s - 1).start())

        @pl.when(outer)
        def _():
            when(s == 0, tell_ring, 2)
            when(s == 8, hear_ring, 2)
            when(s == 13, tell_ring, 3)
            within(u, LAG2_FIRST, first, 1)

        @pl.when(hub)
        def _():
            within(u, LAG2_PAIR, paired, 1)
            within(u, LAG2_TOTAL, totalled, 1)

        return carry

    def drain(u, carry):
        done = samples + lag_mlp + 1

        @pl.when(outer)
        def _():
            when(u == LAG2_FIRST + samples - 1, hear_ring, 3)
            within(u, LAG2_FIRST, first, 1)
            when(u >= LAG2_SHARE, shared, 1, u - LAG2_SHARE)

        @pl.when(hub)
        def _():
            within(u, LAG2_PAIR, paired, 1)
            within(u, LAG2_TOTAL, totalled, 1)

        when(u == done, w_first)
        when(u == done, swap.wait_recv)
        when(u == done + 2, w_along_xy)
        when(u == done + 9, w_along_z)
        s = u - LAG2_SHARE - 1

        @pl.when((s >= 0) & (s % 2 == 0))
        def _():
            proj_some([s, s + 1])
            when(s >= 2, final, [s - 2, s - 1])

        return carry

    lax.fori_loop(0, lag_mlp, fill, 0)
    lax.fori_loop(0, samples + 1, middle, 0)
    lax.fori_loop(samples + lag_mlp + 1, samples - 2 + LAG2_SHARE, drain, 0)
    last = [samples - 2, samples - 1]

    @pl.when(outer)
    def _():
        shared(1, samples - 2)

    proj_some([samples - 2])

    @pl.when(outer)
    def _():
        shared(1, samples - 1)

    here = p_land.at[pl.ds(dp, 1)]
    for i in range(2):
        proj = (proj_acc[i] + proj_of(i == 0, [samples - 1])).reshape(16, 8, 256)
        p_mine[i] = jnp.concatenate([proj[..., :128], proj[..., 128:]], axis=1).astype(BF)
    for dh, dy, xi, i in itertools.product((1, 0), (2, 1, 3, 0), (0, 1), (0, 1)):
        there = xi * 8 + ((y + dy) % 4) * 2 + (hi + dh) % 2
        core = c if i == 0 else 1 - c
        copy = send(p_mine.at[i, pl.ds(there, 1)], here, pss, prs, (half * 16 + there, z * 2 + core))
        if dh == 0 and dy == 0 and i == 0:
            pl.when(half * 2 + xi != x)(copy.start)
        else:
            copy.start()

    @pl.when(hi_half == half)
    def _():
        p_land[dp] = p_mine[0, dp % 16]

    def p_some(count):
        return send(p_land.at[pl.ds(0, count)], p_land.at[pl.ds(0, count)], pss, prs, buddy)

    final([samples - 4, samples - 3])
    for s in last:
        share(1, s).wait_recv()
    grad_of(last)
    w_share()

    for q in range(2):
        sent = [send(chip.at[q], land_b.at[q], ssem.at[q, k], rsem.at[q, 0, 0], buddy) for k in range(4)]
        for k in (0, 1, 3):
            sent[k].wait_send()

        @pl.when(hub)
        def _():
            sent[2].wait_send()
    w_core.wait_send()
    w_xy_all.wait_send()

    @pl.when(c != hi)
    def _():
        w_z_some(4).wait_send()
        w_last.wait_recv()

    @pl.when(c == hi)
    def _():
        w_z_some(3).wait_send()
        w_last.wait_send()

    hg_ref[:, :256] = w_all[:8, :256] * mlp_scale
    hg_ref[:, 256:] = w_all[8:, :256] * mlp_scale
    og_ref[...] = w_all[:, 256:] * mlp_scale
    pl.when(hi_half == half)(lambda: p_some(31).wait_recv())
    pl.when(hi_half != half)(lambda: p_some(32).wait_recv())
    total = p_land[0].astype(F32)
    for d in range(1, 32):
        total += p_land[d].astype(F32)
    pg_ref[:, :128] = total[:8] * proj_scale
    pg_ref[:, 128:] = total[8:] * proj_scale
    swap.wait_send()
    pl.when(hi_half == half)(lambda: p_some(31).wait_send())
    pl.when(hi_half != half)(lambda: p_some(32).wait_send())


def finish(*refs):
    count = (len(refs) - 1) // 2
    copies = [pltpu.make_async_copy(refs[i], refs[count + i], refs[-1].at[i]) for i in range(count)]
    for copy in copies:
        copy.start()
    for copy in copies:
        copy.wait()


def local(embeds, proj_weight, hidden_weight, out_weight, cotangent):
    n, f, d = embeds.shape
    k = proj_weight.shape[1]
    h = hidden_weight.shape[1]
    dp_count = lax.axis_size("dp")
    mlp_scale = 4.0 / (n * dp_count)
    proj_scale = 1.0 / (n * dp_count * math.sqrt(d))
    vmem = pltpu.VMEM
    dma = pltpu.SemaphoreType.DMA
    hbm = pl.BlockSpec(memory_space=pltpu.HBM)
    anywhere = pl.BlockSpec(memory_space=pl.ANY)
    inside = pl.BlockSpec(memory_space=pltpu.VMEM)
    shapes = (
        jax.ShapeDtypeStruct((n, f, d), BF),
        jax.ShapeDtypeStruct((8, f), F32),
        jax.ShapeDtypeStruct((8, h), F32),
        jax.ShapeDtypeStruct((16, d), F32),
    )
    results = pl.pallas_call(
        functools.partial(kernel, n, proj_scale, mlp_scale),
        out_shape=tuple(vmem(v.shape, v.dtype) for v in shapes),
        in_specs=[hbm] * 5,
        out_specs=(inside,) * 4,
        scratch_shapes=[
            vmem((n, f, d), BF), vmem((f, k), BF), vmem((k, h), BF), vmem((h, d), BF), vmem((n, f, d), BF),
            vmem((k, f), BF), vmem((h, k), BF), vmem((h, d), BF),
            vmem((2, n, k, d), BF),
            vmem((2, n, k // 2, d), BF),
            vmem((2, n, k // 2, d), BF),
            vmem((2, n, k // 2, d), BF),
            vmem((2, n, k // 2, d), BF),
            vmem((2, n, k // 2, d), BF),
            vmem((2, n, k, d), BF),
            vmem((n, h, f), F32),
            vmem((n, k, f), BF),
            vmem((2, k, f), BF), vmem((2, h, f), BF), vmem((2, h, f), BF),
            vmem((k, h), F32), vmem((h, d), F32), vmem((2, k // 2, f), F32),
            vmem((16, 2, 16, 384), BF), vmem((16, 16, 384), BF), vmem((16, 16, 384), BF),
            vmem((16, 16, 384), BF), vmem((16, 384), BF), vmem((8, 16, 384), BF), vmem((16, 384), F32),
            vmem((2, 16, 16, 128), BF), vmem((32, 16, 128), BF), vmem((n, f, d), BF),
            dma((5,)), dma((2, 5)), dma((2, n, 5)),
            dma((4,)), dma((4,)), dma, dma, pltpu.SemaphoreType.REGULAR((4,)),
        ],
        compiler_params=pltpu.CompilerParams(
            collective_id=0, has_side_effects=True, vmem_limit_bytes=48 * 1024 * 1024
        ),
    )(*[pltpu.with_memory_space_constraint(v, pltpu.HBM) for v in (embeds, proj_weight, hidden_weight, out_weight, cotangent)])
    grad, proj, hid, out = pl.pallas_call(
        finish,
        out_shape=shapes,
        in_specs=[inside] * 4,
        out_specs=(hbm,) * 4,
        scratch_shapes=[dma((4,))],
        compiler_params=pltpu.CompilerParams(vmem_limit_bytes=48 * 1024 * 1024),
    )(*results)
    return grad, proj.T, hid, out


def solution(mesh):
    placed = (P("dp", "feat", None), P("feat", None), P(), P(), P("dp", "feat", None))
    return jax.shard_map(
        local,
        mesh=mesh,
        in_specs=placed,
        out_specs=(P("dp", "feat", None), P("feat", "dp"), P("dp", None), P("dp", None)),
        check_vma=False,
    )
```

```python
import functools
import itertools
import math

import jax
import jax.numpy as jnp
from jax import lax
from jax.experimental import pallas as pl
from jax.experimental.pallas import tpu as pltpu
from jax.sharding import PartitionSpec as P

MESH = pl.DeviceIdType.MESH
BF = jnp.bfloat16
F32 = jnp.float32

LAG_TOTAL = 4
LAG_SHARE = 8
LAG_MLP = 10
LAG_MLP_HUB = 6
LAG2_FIRST = 12
LAG2_PAIR = 16
LAG2_TOTAL = 20
LAG2_SHARE = 27


def nn(a, b):
    return lax.dot_general(a, b, (((1,), (0,)), ((), ())), preferred_element_type=F32)


def nt(a, b):
    return lax.dot_general(a, b, (((1,), (1,)), ((), ())), preferred_element_type=F32)


def tn(a, b):
    return lax.dot_general(a, b, (((0,), (0,)), ((), ())), preferred_element_type=F32)


def kernel(
    samples, proj_scale, mlp_scale, e_hbm, p_hbm, w1_hbm, w2_hbm, c_hbm,
    eg_ref, pg_ref, hg_ref, og_ref,
    e_ref, p_ref, w1_ref, w2_ref, c_ref, pt_ref, w1t_ref, w2h_ref,
    part, land_a, chip, land_b, pair, land_c, full,
    act_cot, icot, inters, acts, pre_cots, hid_acc, out_acc, proj_acc,
    w_mine, w_buddy, w_chip, w_xy, w_plane, w_z, w_all,
    p_mine, p_land,
    e2_ref, load_sem, ssem, rsem, wss, wrs, pss, prs, relay,
):
    pairs = samples // 2
    dp, ft = lax.axis_index("dp"), lax.axis_index("feat")
    x, y, hi = dp // 8, (dp // 2) % 4, dp % 2
    z, c = ft // 2, ft % 2
    hub = (z == 1) | (z == 2)
    outer = (z == 0) | (z == 3)
    half = (c + z) % 2
    hi_half = dp // 16
    other = pl.ds(pl.multiple_of((1 - half) * 128, 128), 128)
    mine = pl.ds(pl.multiple_of(half * 128, 128), 128)
    buddy = (dp, z * 2 + 1 - c)
    edge_z = jnp.where(z == 0, 1, jnp.where(z == 1, 0, jnp.where(z == 2, 3, 2)))
    edge = (dp, edge_z * 2 + 1 - c)
    across = (dp, (3 - z) * 2 + 1 - c)
    ring = (dp + 1 - 2 * hi, (3 - z) * 2 + c)
    third = (jnp.where(hub, dp, dp + 1 - 2 * hi), (3 - z) * 2 + jnp.where(hub, 1 - c, c))
    sides = [
        (((x + 1) % 4) * 8 + y * 2 + hi, ft),
        (((x + 3) % 4) * 8 + y * 2 + hi, ft),
        (x * 8 + ((y + 1) % 4) * 2 + hi, ft),
        (x * 8 + ((y + 3) % 4) * 2 + hi, ft),
    ]

    opposite = [(((x + 2) % 4) * 8 + y * 2 + hi, ft), (x * 8 + ((y + 2) % 4) * 2 + hi, ft)]

    barrier = pltpu.get_barrier_semaphore()
    peers = [buddy, edge, third] + sides
    for peer in peers:
        pl.semaphore_signal(barrier, inc=1, device_id=peer, device_id_type=MESH)

    loads = [
        pltpu.make_async_copy(src, dst, load_sem.at[i])
        for i, (src, dst) in enumerate(
            ((p_hbm, p_ref), (e_hbm, e_ref), (w1_hbm, w1_ref), (w2_hbm, w2_ref), (c_hbm, c_ref))
        )
    ]
    for load in loads[:2]:
        load.start()

    def tell(r):
        for peer in (sides, opposite)[r]:
            pl.semaphore_signal(relay.at[r], inc=1, device_id=peer, device_id_type=MESH)

    def hear(r):
        pl.semaphore_wait(relay.at[r], (4, 2)[r])

    def tell_ring(r):
        pl.semaphore_signal(relay.at[r], inc=1, device_id=ring, device_id_type=MESH)

    def hear_ring(r):
        pl.semaphore_wait(relay.at[r], 1)

    def send(src, dst, s_sem, r_sem, device):
        return pltpu.make_async_remote_copy(
            src_ref=src, dst_ref=dst, send_sem=s_sem, recv_sem=r_sem,
            device_id=device, device_id_type=MESH,
        )

    swap = send(e_ref, e2_ref, ssem.at[0, 4], rsem.at[0, 0, 4], buddy)

    def to_buddy(q, s):
        return send(part.at[q, s, other], land_a.at[q, s], ssem.at[q, 0], rsem.at[q, s, 0], buddy)

    def to_hub(q, s):
        return send(chip.at[q, s], land_b.at[q, s], ssem.at[q, 1], rsem.at[q, s, 1], edge)

    def to_across(q, s):
        return send(pair.at[q, s], land_c.at[q, s], ssem.at[q, 1], rsem.at[q, s, 2], across)

    def to_outer(q, s):
        ref = full.at[q, s, mine]
        return send(ref, ref, ssem.at[q, 2], rsem.at[q, s, 1], edge)

    def share(q, s):
        ref = full.at[q, s, mine]
        return send(ref, ref, ssem.at[q, 3], rsem.at[q, s, 3], buddy)

    def first(q, s):
        to_buddy(q, s).wait_recv()
        chip[q, s] = (part[q, s, mine].astype(F32) + land_a[q, s].astype(F32)).astype(BF)
        to_hub(q, s).start()

    def paired(q, s):
        to_buddy(q, s).wait_recv()
        to_hub(q, s).wait_recv()
        total = part[q, s, mine].astype(F32) + land_a[q, s].astype(F32) + land_b[q, s].astype(F32)
        pair[q, s] = total.astype(BF)
        to_across(q, s).start()

    def totalled(q, s):
        to_across(q, s).wait_recv()
        full[q, s, mine] = (pair[q, s].astype(F32) + land_c[q, s].astype(F32)).astype(BF)
        to_outer(q, s).start()
        share(q, s).start()

    def shared(q, s):
        to_outer(q, s).wait_recv()
        share(q, s).start()

    loads[0].wait()
    pt_ref[...] = p_ref[...].T
    loads[1].wait()
    for load in loads[2:]:
        load.start()

    def start_samples(i, carry):
        for s in [4 * i + j for j in range(4)]:
            part[0, s] = nn(pt_ref[...], e_ref[s]).astype(BF)
        return carry

    def send_samples(s, carry):
        to_buddy(0, s).start()
        return carry

    lax.fori_loop(0, samples // 4, start_samples, 0)
    pl.semaphore_wait(barrier, len(peers))
    lax.fori_loop(0, samples, send_samples, 0)
    tell(0)
    swap.start()

    def first_samples(low, high):
        def body(s, carry):
            first(0, s)
            return carry

        lax.fori_loop(low, high, body, 0)

    @pl.when(outer)
    def _():
        first_samples(0, 6)

    hid_acc[...] = jnp.zeros_like(hid_acc)
    out_acc[...] = jnp.zeros_like(out_acc)
    proj_acc[...] = jnp.zeros_like(proj_acc)
    for ref in (inters, acts, pre_cots):
        ref[...] = jnp.zeros_like(ref)
    for load in loads[2:]:
        load.wait()
    w1t_ref[...] = (w1_ref[...].T.astype(F32) * 0.5).astype(BF)
    w2h_ref[...] = (w2_ref[...].astype(F32) * 0.5).astype(BF)

    def act_cots(i, carry):
        for s in (2 * i, 2 * i + 1):
            act_cot[s] = nt(w2h_ref[...], c_ref[s])
        return carry

    lax.fori_loop(0, pairs, act_cots, 0)

    @pl.when(outer)
    def _():
        hear(0)
        tell(1)
        first_samples(6, 12)
        hear(1)
        first_samples(12, samples)

    def mlp(s, now, before):
        r = jnp.maximum(s - 1, 0)
        s = jnp.minimum(s, samples - 1)
        inter_cot = nn(w1_ref[...], pre_cots[before]).astype(BF)
        icot[r] = inter_cot
        inter = nt(full[0, s], e_ref[s]).astype(BF)
        hid_acc[...] += nt(inters[before], pre_cots[before])
        u = nn(w1t_ref[...], inter)
        out_acc[...] += nn(acts[before], c_ref[r])
        t = jnp.tanh(u)
        p = 1.0 + t
        a = u * p
        inters[now] = inter
        acts[now] = a.astype(BF)
        pre_cots[now] = (act_cot[s] * (p + a * (1.0 - t))).astype(BF)
        part[1, r] = nn(inter_cot, e_ref[r]).astype(BF)

    def grad_of(both):
        for s in both:
            total = tn(icot[s], full[0, s]) + nn(p_ref[...], full[1, s])
            eg_ref[s] = (c_ref[s].astype(F32) + total).astype(BF)

    def proj_of(own, both):
        emb = e_ref if own else e2_ref
        return sum(nt(full[1, s, mine], emb[s]) for s in both)

    def proj_some(both):
        for i in range(2):
            proj_acc[i] += proj_of(i == 0, both)

    def final(both):
        for s in both:
            share(1, s).wait_recv()
        grad_of(both)

    w_core = send(w_mine.at[:, 1 - c], w_buddy, wss.at[0], wrs.at[0], buddy)
    place = x * 4 + y
    w_xyc = []
    for d in range(1, 16):
        there = (place + d) % 16
        w_xyc.append(send(w_chip.at[there], w_xy.at[d], wss.at[1], wrs.at[1], (there * 2 + hi, ft)))
    w_xy_all = send(w_chip.at[pl.ds(0, 15)], w_xy.at[pl.ds(1, 15)], wss.at[1], wrs.at[1], buddy)
    slot = hi * 4 + z
    w_zc = [
        send(w_plane, w_z.at[slot], wss.at[2], wrs.at[2], (place * 2 + c, ((z + d) % 4) * 2 + c))
        for d in range(4)
    ]

    def w_z_some(count):
        return send(w_z.at[pl.ds(0, count)], w_z.at[pl.ds(0, count)], wss.at[2], wrs.at[2], buddy)

    w_last = send(w_all, w_all, wss.at[3], wrs.at[3], buddy)

    def w_first():
        hid = hid_acc[...].reshape(16, 2, 8, 512)
        hid = jnp.concatenate([hid[..., :256], hid[..., 256:]], axis=2)
        w_mine[..., :256] = hid.astype(BF)
        w_mine[..., 256:] = out_acc[...].reshape(16, 2, 16, 128).astype(BF)
        w_core.start()

    def w_along_xy():
        w_core.wait_recv()
        w_chip[...] = (w_mine[:, c].astype(F32) + w_buddy[...].astype(F32)).astype(BF)
        for copy in w_xyc:
            copy.start()

    def w_along_z():
        w_xy_all.wait_recv()
        total = w_chip[place].astype(F32)
        for d in range(1, 16):
            total += w_xy[d].astype(F32)
        w_plane[...] = total.astype(BF)
        for copy in w_zc[1:]:
            copy.start()

        @pl.when(c != hi)
        def _():
            w_zc[0].start()

        @pl.when(c == hi)
        def _():
            w_z[slot] = total.astype(BF)

    def w_share():
        @pl.when(c == hi)
        def _():
            w_z_some(7).wait_recv()
            total = w_z[0].astype(F32)
            for d in range(1, 8):
                total += w_z[d].astype(F32)
            w_all[...] = total
            w_last.start()

    def when(condition, act, *args):
        pl.when(condition)(lambda: act(*args))

    def within(u, lag, act, *args):
        when((u >= lag) & (u < lag + samples), act, *args, u - lag)

    lag_mlp = jnp.where(hub, LAG_MLP_HUB, LAG_MLP)

    def fill(u, carry):
        @pl.when(hub)
        def _():
            when(u == 0, hear, 0)
            when(u == 0, tell, 1)
            paired(0, u)
            when(u >= LAG_TOTAL, totalled, 0, u - LAG_TOTAL)

        when(outer & (u >= LAG_SHARE), shared, 0, u - LAG_SHARE)
        return carry

    def middle(s, carry):
        u = s + lag_mlp
        now = s % 2

        @pl.when(hub)
        def _():
            when(u == 8, hear, 1)
            within(u, 0, paired, 0)
            within(u, LAG_TOTAL, totalled, 0)

        when(s < samples, lambda: share(0, s).wait_recv())
        mlp(s, now, 1 - now)
        when(s > 0, lambda: to_buddy(1, s - 1).start())

        @pl.when(outer)
        def _():
            within(u, LAG_SHARE, shared, 0)
            when(s == 0, tell_ring, 2)
            when(s == 8, hear_ring, 2)
            when(s == 13, tell_ring, 3)
            within(u, LAG2_FIRST, first, 1)

        @pl.when(hub)
        def _():
            within(u, LAG2_PAIR, paired, 1)
            within(u, LAG2_TOTAL, totalled, 1)

        return carry

    def drain(u, carry):
        done = samples + lag_mlp + 1

        @pl.when(outer)
        def _():
            when(u == LAG2_FIRST + samples - 1, hear_ring, 3)
            within(u, LAG2_FIRST, first, 1)
            when(u >= LAG2_SHARE, shared, 1, u - LAG2_SHARE)

        @pl.when(hub)
        def _():
            within(u, LAG2_PAIR, paired, 1)
            within(u, LAG2_TOTAL, totalled, 1)

        when(u == done, w_first)
        when(u == done, swap.wait_recv)
        when(u == done + 3, w_along_xy)
        when(u == done + 10, w_along_z)
        s = u - LAG2_SHARE - 1

        @pl.when((s >= 0) & (s % 2 == 0))
        def _():
            proj_some([s, s + 1])

        return carry

    lax.fori_loop(0, lag_mlp, fill, 0)
    lax.fori_loop(0, samples + 1, middle, 0)
    lax.fori_loop(samples + lag_mlp + 1, samples - 2 + LAG2_SHARE, drain, 0)

    @pl.when(outer)
    def _():
        shared(1, samples - 2)

    proj_some([samples - 2])

    @pl.when(outer)
    def _():
        shared(1, samples - 1)

    here = p_land.at[pl.ds(dp, 1)]
    for i in range(2):
        proj = (proj_acc[i] + proj_of(i == 0, [samples - 1])).reshape(16, 8, 256)
        p_mine[i] = jnp.concatenate([proj[..., :128], proj[..., 128:]], axis=1).astype(BF)
    for dh, dy, xi, i in itertools.product((1, 0), (2, 1, 3, 0), (0, 1), (0, 1)):
        there = xi * 8 + ((y + dy) % 4) * 2 + (hi + dh) % 2
        core = c if i == 0 else 1 - c
        copy = send(p_mine.at[i, pl.ds(there, 1)], here, pss, prs, (half * 16 + there, z * 2 + core))
        if dh == 0 and dy == 0 and i == 0:
            pl.when(half * 2 + xi != x)(copy.start)
        else:
            copy.start()

    @pl.when(hi_half == half)
    def _():
        p_land[dp] = p_mine[0, dp % 16]

    def p_some(count):
        return send(p_land.at[pl.ds(0, count)], p_land.at[pl.ds(0, count)], pss, prs, buddy)

    def finals(i, carry):
        final([2 * i, 2 * i + 1])
        return carry

    lax.fori_loop(0, pairs // 2, finals, 0)
    w_share()
    lax.fori_loop(pairs // 2, pairs, finals, 0)

    for q in range(2):
        sent = [send(chip.at[q], land_b.at[q], ssem.at[q, k], rsem.at[q, 0, 0], buddy) for k in range(4)]
        for k in (0, 1, 3):
            sent[k].wait_send()

        @pl.when(hub)
        def _():
            sent[2].wait_send()
    w_core.wait_send()
    w_xy_all.wait_send()

    @pl.when(c != hi)
    def _():
        w_z_some(4).wait_send()
        w_last.wait_recv()

    @pl.when(c == hi)
    def _():
        w_z_some(3).wait_send()
        w_last.wait_send()

    hg_ref[:, :256] = w_all[:8, :256] * mlp_scale
    hg_ref[:, 256:] = w_all[8:, :256] * mlp_scale
    og_ref[...] = w_all[:, 256:] * mlp_scale
    pl.when(hi_half == half)(lambda: p_some(31).wait_recv())
    pl.when(hi_half != half)(lambda: p_some(32).wait_recv())
    total = p_land[0].astype(F32)
    for d in range(1, 32):
        total += p_land[d].astype(F32)
    pg_ref[:, :128] = total[:8] * proj_scale
    pg_ref[:, 128:] = total[8:] * proj_scale
    swap.wait_send()
    pl.when(hi_half == half)(lambda: p_some(31).wait_send())
    pl.when(hi_half != half)(lambda: p_some(32).wait_send())


def finish(*refs):
    count = (len(refs) - 1) // 2
    copies = [pltpu.make_async_copy(refs[i], refs[count + i], refs[-1].at[i]) for i in range(count)]
    for copy in copies:
        copy.start()
    for copy in copies:
        copy.wait()


def local(embeds, proj_weight, hidden_weight, out_weight, cotangent):
    n, f, d = embeds.shape
    k = proj_weight.shape[1]
    h = hidden_weight.shape[1]
    dp_count = lax.axis_size("dp")
    mlp_scale = 4.0 / (n * dp_count)
    proj_scale = 1.0 / (n * dp_count * math.sqrt(d))
    vmem = pltpu.VMEM
    dma = pltpu.SemaphoreType.DMA
    hbm = pl.BlockSpec(memory_space=pltpu.HBM)
    anywhere = pl.BlockSpec(memory_space=pl.ANY)
    inside = pl.BlockSpec(memory_space=pltpu.VMEM)
    shapes = (
        jax.ShapeDtypeStruct((n, f, d), BF),
        jax.ShapeDtypeStruct((8, f), F32),
        jax.ShapeDtypeStruct((8, h), F32),
        jax.ShapeDtypeStruct((16, d), F32),
    )
    results = pl.pallas_call(
        functools.partial(kernel, n, proj_scale, mlp_scale),
        out_shape=tuple(vmem(v.shape, v.dtype) for v in shapes),
        in_specs=[hbm] * 5,
        out_specs=(inside,) * 4,
        scratch_shapes=[
            vmem((n, f, d), BF), vmem((f, k), BF), vmem((k, h), BF), vmem((h, d), BF), vmem((n, f, d), BF),
            vmem((k, f), BF), vmem((h, k), BF), vmem((h, d), BF),
            vmem((2, n, k, d), BF),
            vmem((2, n, k // 2, d), BF),
            vmem((2, n, k // 2, d), BF),
            vmem((2, n, k // 2, d), BF),
            vmem((2, n, k // 2, d), BF),
            vmem((2, n, k // 2, d), BF),
            vmem((2, n, k, d), BF),
            vmem((n, h, f), F32),
            vmem((n, k, f), BF),
            vmem((2, k, f), BF), vmem((2, h, f), BF), vmem((2, h, f), BF),
            vmem((k, h), F32), vmem((h, d), F32), vmem((2, k // 2, f), F32),
            vmem((16, 2, 16, 384), BF), vmem((16, 16, 384), BF), vmem((16, 16, 384), BF),
            vmem((16, 16, 384), BF), vmem((16, 384), BF), vmem((8, 16, 384), BF), vmem((16, 384), F32),
            vmem((2, 16, 16, 128), BF), vmem((32, 16, 128), BF), vmem((n, f, d), BF),
            dma((5,)), dma((2, 5)), dma((2, n, 5)),
            dma((4,)), dma((4,)), dma, dma, pltpu.SemaphoreType.REGULAR((4,)),
        ],
        compiler_params=pltpu.CompilerParams(
            collective_id=0, has_side_effects=True, vmem_limit_bytes=48 * 1024 * 1024
        ),
    )(*[pltpu.with_memory_space_constraint(v, pltpu.HBM) for v in (embeds, proj_weight, hidden_weight, out_weight, cotangent)])
    grad, proj, hid, out = pl.pallas_call(
        finish,
        out_shape=shapes,
        in_specs=[inside] * 4,
        out_specs=(hbm,) * 4,
        scratch_shapes=[dma((4,))],
        compiler_params=pltpu.CompilerParams(vmem_limit_bytes=48 * 1024 * 1024),
    )(*results)
    return grad, proj.T, hid, out


def solution(mesh):
    placed = (P("dp", "feat", None), P("feat", None), P(), P(), P("dp", "feat", None))
    return jax.shard_map(
        local,
        mesh=mesh,
        in_specs=placed,
        out_specs=(P("dp", "feat", None), P("feat", "dp"), P("dp", None), P("dp", None)),
        check_vma=False,
    )
```

```python
import functools
import itertools
import math

import jax
import jax.numpy as jnp
from jax import lax
from jax.experimental import pallas as pl
from jax.experimental.pallas import tpu as pltpu
from jax.sharding import PartitionSpec as P

MESH = pl.DeviceIdType.MESH
BF = jnp.bfloat16
F32 = jnp.float32

LAG_TOTAL = 4
LAG_SHARE = 8
LAG_MLP = 10
LAG_MLP_HUB = 6
LAG2_FIRST = 12
LAG2_PAIR = 16
LAG2_TOTAL = 20
LAG2_SHARE = 27


def nn(a, b):
    return lax.dot_general(a, b, (((1,), (0,)), ((), ())), preferred_element_type=F32)


def nt(a, b):
    return lax.dot_general(a, b, (((1,), (1,)), ((), ())), preferred_element_type=F32)


def tn(a, b):
    return lax.dot_general(a, b, (((0,), (0,)), ((), ())), preferred_element_type=F32)


def kernel(
    samples, proj_scale, mlp_scale, e_hbm, p_hbm, w1_hbm, w2_hbm, c_hbm,
    eg_ref, pg_ref, hg_ref, og_ref,
    e_ref, p_ref, w1_ref, w2_ref, c_ref, pt_ref, w1t_ref, w2h_ref,
    part, land_a, chip, land_b, pair, land_c, full,
    act_cot, icot, inters, acts, pre_cots, hid_acc, out_acc, proj_acc,
    w_mine, w_buddy, w_chip, w_xy, w_plane, w_z, w_all,
    p_mine, p_land,
    e2_ref, load_sem, ssem, rsem, wss, wrs, pss, prs, relay,
):
    pairs = samples // 2
    dp, ft = lax.axis_index("dp"), lax.axis_index("feat")
    x, y, hi = dp // 8, (dp // 2) % 4, dp % 2
    z, c = ft // 2, ft % 2
    hub = (z == 1) | (z == 2)
    outer = (z == 0) | (z == 3)
    half = (c + z) % 2
    hi_half = dp // 16
    other = pl.ds(pl.multiple_of((1 - half) * 128, 128), 128)
    mine = pl.ds(pl.multiple_of(half * 128, 128), 128)
    buddy = (dp, z * 2 + 1 - c)
    edge_z = jnp.where(z == 0, 1, jnp.where(z == 1, 0, jnp.where(z == 2, 3, 2)))
    edge = (dp, edge_z * 2 + 1 - c)
    across = (dp, (3 - z) * 2 + 1 - c)
    ring = (dp + 1 - 2 * hi, (3 - z) * 2 + c)
    third = (jnp.where(hub, dp, dp + 1 - 2 * hi), (3 - z) * 2 + jnp.where(hub, 1 - c, c))
    sides = [
        (((x + 1) % 4) * 8 + y * 2 + hi, ft),
        (((x + 3) % 4) * 8 + y * 2 + hi, ft),
        (x * 8 + ((y + 1) % 4) * 2 + hi, ft),
        (x * 8 + ((y + 3) % 4) * 2 + hi, ft),
    ]

    opposite = [(((x + 2) % 4) * 8 + y * 2 + hi, ft), (x * 8 + ((y + 2) % 4) * 2 + hi, ft)]

    barrier = pltpu.get_barrier_semaphore()
    peers = sides + [edge, third, buddy]
    for peer in peers:
        pl.semaphore_signal(barrier, inc=1, device_id=peer, device_id_type=MESH)

    loads = [
        pltpu.make_async_copy(src, dst, load_sem.at[i])
        for i, (src, dst) in enumerate(
            ((p_hbm, p_ref), (e_hbm, e_ref), (w1_hbm, w1_ref), (w2_hbm, w2_ref), (c_hbm, c_ref))
        )
    ]
    for load in loads[:2]:
        load.start()

    def tell(r):
        for peer in (sides, opposite)[r]:
            pl.semaphore_signal(relay.at[r], inc=1, device_id=peer, device_id_type=MESH)

    def hear(r):
        pl.semaphore_wait(relay.at[r], (4, 2)[r])

    def tell_ring(r):
        pl.semaphore_signal(relay.at[r], inc=1, device_id=ring, device_id_type=MESH)

    def hear_ring(r):
        pl.semaphore_wait(relay.at[r], 1)

    def send(src, dst, s_sem, r_sem, device):
        return pltpu.make_async_remote_copy(
            src_ref=src, dst_ref=dst, send_sem=s_sem, recv_sem=r_sem,
            device_id=device, device_id_type=MESH,
        )

    swap = send(e_ref, e2_ref, ssem.at[0, 4], rsem.at[0, 0, 4], buddy)

    def to_buddy(q, s):
        return send(part.at[q, s, other], land_a.at[q, s], ssem.at[q, 0], rsem.at[q, s, 0], buddy)

    def to_hub(q, s):
        return send(chip.at[q, s], land_b.at[q, s], ssem.at[q, 1], rsem.at[q, s, 1], edge)

    def to_across(q, s):
        return send(pair.at[q, s], land_c.at[q, s], ssem.at[q, 1], rsem.at[q, s, 2], across)

    def to_outer(q, s):
        ref = full.at[q, s, mine]
        return send(ref, ref, ssem.at[q, 2], rsem.at[q, s, 1], edge)

    def share(q, s):
        ref = full.at[q, s, mine]
        return send(ref, ref, ssem.at[q, 3], rsem.at[q, s, 3], buddy)

    def first(q, s):
        to_buddy(q, s).wait_recv()
        chip[q, s] = (part[q, s, mine].astype(F32) + land_a[q, s].astype(F32)).astype(BF)
        to_hub(q, s).start()

    def paired(q, s):
        to_buddy(q, s).wait_recv()
        to_hub(q, s).wait_recv()
        total = part[q, s, mine].astype(F32) + land_a[q, s].astype(F32) + land_b[q, s].astype(F32)
        pair[q, s] = total.astype(BF)
        to_across(q, s).start()

    def totalled(q, s):
        to_across(q, s).wait_recv()
        full[q, s, mine] = (pair[q, s].astype(F32) + land_c[q, s].astype(F32)).astype(BF)
        to_outer(q, s).start()
        share(q, s).start()

    def shared(q, s):
        to_outer(q, s).wait_recv()
        share(q, s).start()

    loads[0].wait()
    pt_ref[...] = p_ref[...].T
    loads[1].wait()
    for load in loads[2:]:
        load.start()

    def start_samples(i, carry):
        for s in [4 * i + j for j in range(4)]:
            part[0, s] = nn(pt_ref[...], e_ref[s]).astype(BF)
        return carry

    def send_samples(s, carry):
        to_buddy(0, s).start()
        return carry

    lax.fori_loop(0, samples // 4, start_samples, 0)
    pl.semaphore_wait(barrier, len(peers))
    lax.fori_loop(0, samples, send_samples, 0)
    tell(0)
    swap.start()

    def first_samples(low, high):
        def body(s, carry):
            first(0, s)
            return carry

        lax.fori_loop(low, high, body, 0)

    @pl.when(outer)
    def _():
        first_samples(0, 6)

    hid_acc[...] = jnp.zeros_like(hid_acc)
    out_acc[...] = jnp.zeros_like(out_acc)
    proj_acc[...] = jnp.zeros_like(proj_acc)
    for ref in (inters, acts, pre_cots):
        ref[...] = jnp.zeros_like(ref)
    for load in loads[2:]:
        load.wait()
    w1t_ref[...] = (w1_ref[...].T.astype(F32) * 0.5).astype(BF)
    w2h_ref[...] = (w2_ref[...].astype(F32) * 0.5).astype(BF)

    def act_cots(i, carry):
        for s in (2 * i, 2 * i + 1):
            act_cot[s] = nt(w2h_ref[...], c_ref[s])
        return carry

    lax.fori_loop(0, pairs, act_cots, 0)

    @pl.when(outer)
    def _():
        hear(0)
        tell(1)
        first_samples(6, 12)
        hear(1)
        first_samples(12, samples)

    def mlp(s, now, before):
        r = jnp.maximum(s - 1, 0)
        s = jnp.minimum(s, samples - 1)
        inter_cot = nn(w1_ref[...], pre_cots[before]).astype(BF)
        icot[r] = inter_cot
        inter = nt(full[0, s], e_ref[s]).astype(BF)
        hid_acc[...] += nt(inters[before], pre_cots[before])
        u = nn(w1t_ref[...], inter)
        out_acc[...] += nn(acts[before], c_ref[r])
        t = jnp.tanh(u)
        p = 1.0 + t
        a = u * p
        inters[now] = inter
        acts[now] = a.astype(BF)
        pre_cots[now] = (act_cot[s] * (p + a * (1.0 - t))).astype(BF)
        part[1, r] = nn(inter_cot, e_ref[r]).astype(BF)

    def grad_of(both):
        for s in both:
            total = tn(icot[s], full[0, s]) + nn(p_ref[...], full[1, s])
            eg_ref[s] = (c_ref[s].astype(F32) + total).astype(BF)

    def proj_of(own, both):
        emb = e_ref if own else e2_ref
        return sum(nt(full[1, s, mine], emb[s]) for s in both)

    def proj_some(both):
        for i in range(2):
            proj_acc[i] += proj_of(i == 0, both)

    def final(both):
        for s in both:
            share(1, s).wait_recv()
        grad_of(both)

    w_core = send(w_mine.at[:, 1 - c], w_buddy, wss.at[0], wrs.at[0], buddy)
    place = x * 4 + y
    w_xyc = []
    for d in range(1, 16):
        there = (place + d) % 16
        w_xyc.append(send(w_chip.at[there], w_xy.at[d], wss.at[1], wrs.at[1], (there * 2 + hi, ft)))
    w_xy_all = send(w_chip.at[pl.ds(0, 15)], w_xy.at[pl.ds(1, 15)], wss.at[1], wrs.at[1], buddy)
    slot = hi * 4 + z
    w_zc = [
        send(w_plane, w_z.at[slot], wss.at[2], wrs.at[2], (place * 2 + c, ((z + d) % 4) * 2 + c))
        for d in range(4)
    ]

    def w_z_some(count):
        return send(w_z.at[pl.ds(0, count)], w_z.at[pl.ds(0, count)], wss.at[2], wrs.at[2], buddy)

    w_last = send(w_all, w_all, wss.at[3], wrs.at[3], buddy)

    def w_first():
        hid = hid_acc[...].reshape(16, 2, 8, 512)
        hid = jnp.concatenate([hid[..., :256], hid[..., 256:]], axis=2)
        w_mine[..., :256] = hid.astype(BF)
        w_mine[..., 256:] = out_acc[...].reshape(16, 2, 16, 128).astype(BF)
        w_core.start()

    def w_along_xy():
        w_core.wait_recv()
        w_chip[...] = (w_mine[:, c].astype(F32) + w_buddy[...].astype(F32)).astype(BF)
        for copy in w_xyc:
            copy.start()

    def w_along_z():
        w_xy_all.wait_recv()
        total = w_chip[place].astype(F32)
        for d in range(1, 16):
            total += w_xy[d].astype(F32)
        w_plane[...] = total.astype(BF)
        for copy in w_zc[1:]:
            copy.start()

        @pl.when(c != hi)
        def _():
            w_zc[0].start()

        @pl.when(c == hi)
        def _():
            w_z[slot] = total.astype(BF)

    def w_share():
        @pl.when(c == hi)
        def _():
            w_z_some(7).wait_recv()
            total = w_z[0].astype(F32)
            for d in range(1, 8):
                total += w_z[d].astype(F32)
            w_all[...] = total
            w_last.start()

    def when(condition, act, *args):
        pl.when(condition)(lambda: act(*args))

    def within(u, lag, act, *args):
        when((u >= lag) & (u < lag + samples), act, *args, u - lag)

    lag_mlp = jnp.where(hub, LAG_MLP_HUB, LAG_MLP)

    def fill(u, carry):
        @pl.when(hub)
        def _():
            when(u == 0, hear, 0)
            when(u == 0, tell, 1)
            paired(0, u)
            when(u >= LAG_TOTAL, totalled, 0, u - LAG_TOTAL)

        when(outer & (u >= LAG_SHARE), shared, 0, u - LAG_SHARE)
        return carry

    def middle(s, carry):
        u = s + lag_mlp
        now = s % 2

        @pl.when(hub)
        def _():
            when(u == 8, hear, 1)
            within(u, 0, paired, 0)
            within(u, LAG_TOTAL, totalled, 0)

        when(s < samples, lambda: share(0, s).wait_recv())
        mlp(s, now, 1 - now)
        when(s > 0, lambda: to_buddy(1, s - 1).start())

        @pl.when(outer)
        def _():
            within(u, LAG_SHARE, shared, 0)
            when(s == 0, tell_ring, 2)
            when(s == 8, hear_ring, 2)
            when(s == 12, tell_ring, 3)
            within(u, LAG2_FIRST, first, 1)

        @pl.when(hub)
        def _():
            within(u, LAG2_PAIR, paired, 1)
            within(u, LAG2_TOTAL, totalled, 1)

        return carry

    def drain(u, carry):
        done = samples + lag_mlp + 1

        @pl.when(outer)
        def _():
            when(u == LAG2_FIRST + samples - 1, hear_ring, 3)
            within(u, LAG2_FIRST, first, 1)
            when(u >= LAG2_SHARE, shared, 1, u - LAG2_SHARE)

        @pl.when(hub)
        def _():
            within(u, LAG2_PAIR, paired, 1)
            within(u, LAG2_TOTAL, totalled, 1)

        when(u == done, w_first)
        when(u == done, swap.wait_recv)
        when(u == done + 3, w_along_xy)
        when(u == done + 10, w_along_z)
        s = u - LAG2_SHARE - 1

        @pl.when((s >= 0) & (s % 2 == 0))
        def _():
            proj_some([s, s + 1])

        return carry

    lax.fori_loop(0, lag_mlp, fill, 0)
    lax.fori_loop(0, samples + 1, middle, 0)
    lax.fori_loop(samples + lag_mlp + 1, samples - 2 + LAG2_SHARE, drain, 0)

    @pl.when(outer)
    def _():
        shared(1, samples - 2)

    proj_some([samples - 2])

    @pl.when(outer)
    def _():
        shared(1, samples - 1)

    here = p_land.at[pl.ds(dp, 1)]
    for i in range(2):
        proj = (proj_acc[i] + proj_of(i == 0, [samples - 1])).reshape(16, 8, 256)
        p_mine[i] = jnp.concatenate([proj[..., :128], proj[..., 128:]], axis=1).astype(BF)
    for dh, dy, xi, i in itertools.product((1, 0), (2, 1, 3, 0), (0, 1), (0, 1)):
        there = xi * 8 + ((y + dy) % 4) * 2 + (hi + dh) % 2
        core = c if i == 0 else 1 - c
        copy = send(p_mine.at[i, pl.ds(there, 1)], here, pss, prs, (half * 16 + there, z * 2 + core))
        if dh == 0 and dy == 0 and i == 0:
            pl.when(half * 2 + xi != x)(copy.start)
        else:
            copy.start()

    @pl.when(hi_half == half)
    def _():
        p_land[dp] = p_mine[0, dp % 16]

    def p_some(count):
        return send(p_land.at[pl.ds(0, count)], p_land.at[pl.ds(0, count)], pss, prs, buddy)

    def finals(i, carry):
        final([2 * i, 2 * i + 1])
        return carry

    lax.fori_loop(0, pairs // 2, finals, 0)
    w_share()
    lax.fori_loop(pairs // 2, pairs, finals, 0)

    for q in range(2):
        sent = [send(chip.at[q], land_b.at[q], ssem.at[q, k], rsem.at[q, 0, 0], buddy) for k in range(4)]
        for k in (0, 1, 3):
            sent[k].wait_send()

        @pl.when(hub)
        def _():
            sent[2].wait_send()
    w_core.wait_send()
    w_xy_all.wait_send()

    @pl.when(c != hi)
    def _():
        w_z_some(4).wait_send()
        w_last.wait_recv()

    @pl.when(c == hi)
    def _():
        w_z_some(3).wait_send()
        w_last.wait_send()

    hg_ref[:, :256] = w_all[:8, :256] * mlp_scale
    hg_ref[:, 256:] = w_all[8:, :256] * mlp_scale
    og_ref[...] = w_all[:, 256:] * mlp_scale
    pl.when(hi_half == half)(lambda: p_some(31).wait_recv())
    pl.when(hi_half != half)(lambda: p_some(32).wait_recv())
    total = p_land[0].astype(F32)
    for d in range(1, 32):
        total += p_land[d].astype(F32)
    pg_ref[:, :128] = total[:8] * proj_scale
    pg_ref[:, 128:] = total[8:] * proj_scale
    swap.wait_send()
    pl.when(hi_half == half)(lambda: p_some(31).wait_send())
    pl.when(hi_half != half)(lambda: p_some(32).wait_send())


def finish(*refs):
    sem = refs[-1]
    count = (len(refs) - 1) // 2
    rows = refs[0].shape[0] // 4
    pairs = [(refs[0].at[pl.ds(i * rows, rows)], refs[count].at[pl.ds(i * rows, rows)]) for i in range(4)]
    pairs += [(refs[i], refs[count + i]) for i in range(1, count)]
    copies = [pltpu.make_async_copy(src, dst, sem.at[i]) for i, (src, dst) in enumerate(pairs)]
    for copy in copies:
        copy.start()
    for copy in copies:
        copy.wait()


def local(embeds, proj_weight, hidden_weight, out_weight, cotangent):
    n, f, d = embeds.shape
    k = proj_weight.shape[1]
    h = hidden_weight.shape[1]
    dp_count = lax.axis_size("dp")
    mlp_scale = 4.0 / (n * dp_count)
    proj_scale = 1.0 / (n * dp_count * math.sqrt(d))
    vmem = pltpu.VMEM
    dma = pltpu.SemaphoreType.DMA
    hbm = pl.BlockSpec(memory_space=pltpu.HBM)
    anywhere = pl.BlockSpec(memory_space=pl.ANY)
    inside = pl.BlockSpec(memory_space=pltpu.VMEM)
    shapes = (
        jax.ShapeDtypeStruct((n, f, d), BF),
        jax.ShapeDtypeStruct((8, f), F32),
        jax.ShapeDtypeStruct((8, h), F32),
        jax.ShapeDtypeStruct((16, d), F32),
    )
    results = pl.pallas_call(
        functools.partial(kernel, n, proj_scale, mlp_scale),
        out_shape=tuple(vmem(v.shape, v.dtype) for v in shapes),
        in_specs=[hbm] * 5,
        out_specs=(inside,) * 4,
        scratch_shapes=[
            vmem((n, f, d), BF), vmem((f, k), BF), vmem((k, h), BF), vmem((h, d), BF), vmem((n, f, d), BF),
            vmem((k, f), BF), vmem((h, k), BF), vmem((h, d), BF),
            vmem((2, n, k, d), BF),
            vmem((2, n, k // 2, d), BF),
            vmem((2, n, k // 2, d), BF),
            vmem((2, n, k // 2, d), BF),
            vmem((2, n, k // 2, d), BF),
            vmem((2, n, k // 2, d), BF),
            vmem((2, n, k, d), BF),
            vmem((n, h, f), F32),
            vmem((n, k, f), BF),
            vmem((2, k, f), BF), vmem((2, h, f), BF), vmem((2, h, f), BF),
            vmem((k, h), F32), vmem((h, d), F32), vmem((2, k // 2, f), F32),
            vmem((16, 2, 16, 384), BF), vmem((16, 16, 384), BF), vmem((16, 16, 384), BF),
            vmem((16, 16, 384), BF), vmem((16, 384), BF), vmem((8, 16, 384), BF), vmem((16, 384), F32),
            vmem((2, 16, 16, 128), BF), vmem((32, 16, 128), BF), vmem((n, f, d), BF),
            dma((5,)), dma((2, 5)), dma((2, n, 5)),
            dma((4,)), dma((4,)), dma, dma, pltpu.SemaphoreType.REGULAR((4,)),
        ],
        compiler_params=pltpu.CompilerParams(
            collective_id=0, has_side_effects=True, vmem_limit_bytes=48 * 1024 * 1024
        ),
    )(*[pltpu.with_memory_space_constraint(v, pltpu.HBM) for v in (embeds, proj_weight, hidden_weight, out_weight, cotangent)])
    grad, proj, hid, out = pl.pallas_call(
        finish,
        out_shape=shapes,
        in_specs=[inside] * 4,
        out_specs=(hbm,) * 4,
        scratch_shapes=[dma((7,))],
        compiler_params=pltpu.CompilerParams(vmem_limit_bytes=48 * 1024 * 1024),
    )(*results)
    return grad, proj.T, hid, out


def solution(mesh):
    placed = (P("dp", "feat", None), P("feat", None), P(), P(), P("dp", "feat", None))
    return jax.shard_map(
        local,
        mesh=mesh,
        in_specs=placed,
        out_specs=(P("dp", "feat", None), P("feat", "dp"), P("dp", None), P("dp", None)),
        check_vma=False,
    )
```

```python
import functools
import itertools
import math

import jax
import jax.numpy as jnp
from jax import lax
from jax.experimental import pallas as pl
from jax.experimental.pallas import tpu as pltpu
from jax.sharding import PartitionSpec as P

MESH = pl.DeviceIdType.MESH
BF = jnp.bfloat16
F32 = jnp.float32

LAG_TOTAL = 4
LAG_SHARE = 8
LAG_MLP = 10
LAG_MLP_HUB = 6
LAG2_FIRST = 12
LAG2_PAIR = 15
LAG2_TOTAL = 19
LAG2_SHARE = 27


def nn(a, b):
    return lax.dot_general(a, b, (((1,), (0,)), ((), ())), preferred_element_type=F32)


def nt(a, b):
    return lax.dot_general(a, b, (((1,), (1,)), ((), ())), preferred_element_type=F32)


def tn(a, b):
    return lax.dot_general(a, b, (((0,), (0,)), ((), ())), preferred_element_type=F32)


def kernel(
    samples, proj_scale, mlp_scale, e_hbm, p_hbm, w1_hbm, w2_hbm, c_hbm,
    eg_ref, pg_ref, hg_ref, og_ref,
    e_ref, p_ref, w1_ref, w2_ref, c_ref, pt_ref, w1t_ref, w2h_ref,
    part, land_a, chip, land_b, pair, land_c, full,
    act_cot, icot, inters, acts, pre_cots, hid_acc, out_acc, proj_acc,
    w_mine, w_buddy, w_chip, w_xy, w_plane, w_z, w_all,
    p_mine, p_land,
    e2_ref, load_sem, ssem, rsem, wss, wrs, pss, prs, relay,
):
    pairs = samples // 2
    dp, ft = lax.axis_index("dp"), lax.axis_index("feat")
    x, y, hi = dp // 8, (dp // 2) % 4, dp % 2
    z, c = ft // 2, ft % 2
    hub = (z == 1) | (z == 2)
    outer = (z == 0) | (z == 3)
    half = (c + z) % 2
    hi_half = dp // 16
    other = pl.ds(pl.multiple_of((1 - half) * 128, 128), 128)
    mine = pl.ds(pl.multiple_of(half * 128, 128), 128)
    buddy = (dp, z * 2 + 1 - c)
    edge_z = jnp.where(z == 0, 1, jnp.where(z == 1, 0, jnp.where(z == 2, 3, 2)))
    edge = (dp, edge_z * 2 + 1 - c)
    across = (dp, (3 - z) * 2 + 1 - c)
    ring = (dp + 1 - 2 * hi, (3 - z) * 2 + c)
    third = (jnp.where(hub, dp, dp + 1 - 2 * hi), (3 - z) * 2 + jnp.where(hub, 1 - c, c))
    sides = [
        (((x + 1) % 4) * 8 + y * 2 + hi, ft),
        (((x + 3) % 4) * 8 + y * 2 + hi, ft),
        (x * 8 + ((y + 1) % 4) * 2 + hi, ft),
        (x * 8 + ((y + 3) % 4) * 2 + hi, ft),
    ]

    opposite = [(((x + 2) % 4) * 8 + y * 2 + hi, ft), (x * 8 + ((y + 2) % 4) * 2 + hi, ft)]

    barrier = pltpu.get_barrier_semaphore()
    peers = [buddy, edge, third] + sides
    for peer in peers:
        pl.semaphore_signal(barrier, inc=1, device_id=peer, device_id_type=MESH)

    loads = [
        pltpu.make_async_copy(src, dst, load_sem.at[i])
        for i, (src, dst) in enumerate(
            ((p_hbm, p_ref), (e_hbm, e_ref), (w1_hbm, w1_ref), (w2_hbm, w2_ref), (c_hbm, c_ref))
        )
    ]
    for load in loads[:2]:
        load.start()

    def tell(r):
        for peer in (sides, opposite)[r]:
            pl.semaphore_signal(relay.at[r], inc=1, device_id=peer, device_id_type=MESH)

    def hear(r):
        pl.semaphore_wait(relay.at[r], (4, 2)[r])

    def tell_ring(r):
        pl.semaphore_signal(relay.at[r], inc=1, device_id=ring, device_id_type=MESH)

    def hear_ring(r):
        pl.semaphore_wait(relay.at[r], 1)

    def send(src, dst, s_sem, r_sem, device):
        return pltpu.make_async_remote_copy(
            src_ref=src, dst_ref=dst, send_sem=s_sem, recv_sem=r_sem,
            device_id=device, device_id_type=MESH,
        )

    swap = send(e_ref, e2_ref, ssem.at[0, 4], rsem.at[0, 0, 4], buddy)

    def to_buddy(q, s):
        return send(part.at[q, s, other], land_a.at[q, s], ssem.at[q, 0], rsem.at[q, s, 0], buddy)

    def to_hub(q, s):
        return send(chip.at[q, s], land_b.at[q, s], ssem.at[q, 1], rsem.at[q, s, 1], edge)

    def to_across(q, s):
        return send(pair.at[q, s], land_c.at[q, s], ssem.at[q, 1], rsem.at[q, s, 2], across)

    def to_outer(q, s):
        ref = full.at[q, s, mine]
        return send(ref, ref, ssem.at[q, 2], rsem.at[q, s, 1], edge)

    def share(q, s):
        ref = full.at[q, s, mine]
        return send(ref, ref, ssem.at[q, 3], rsem.at[q, s, 3], buddy)

    def first(q, s):
        to_buddy(q, s).wait_recv()
        chip[q, s] = (part[q, s, mine].astype(F32) + land_a[q, s].astype(F32)).astype(BF)
        to_hub(q, s).start()

    def paired(q, s):
        to_buddy(q, s).wait_recv()
        to_hub(q, s).wait_recv()
        total = part[q, s, mine].astype(F32) + land_a[q, s].astype(F32) + land_b[q, s].astype(F32)
        pair[q, s] = total.astype(BF)
        to_across(q, s).start()

    def totalled(q, s):
        to_across(q, s).wait_recv()
        full[q, s, mine] = (pair[q, s].astype(F32) + land_c[q, s].astype(F32)).astype(BF)
        to_outer(q, s).start()
        share(q, s).start()

    def shared(q, s):
        to_outer(q, s).wait_recv()
        share(q, s).start()

    loads[0].wait()
    pt_ref[...] = p_ref[...].T
    loads[1].wait()
    for load in loads[2:]:
        load.start()

    def start_samples(i, carry):
        for s in [4 * i + j for j in range(4)]:
            part[0, s] = nn(pt_ref[...], e_ref[s]).astype(BF)
        return carry

    def send_samples(s, carry):
        to_buddy(0, s).start()
        return carry

    lax.fori_loop(0, samples // 4, start_samples, 0)
    pl.semaphore_wait(barrier, len(peers))
    lax.fori_loop(0, samples, send_samples, 0)
    tell(0)
    swap.start()

    def first_samples(low, high):
        def body(s, carry):
            first(0, s)
            return carry

        lax.fori_loop(low, high, body, 0)

    @pl.when(outer)
    def _():
        first_samples(0, 6)

    hid_acc[...] = jnp.zeros_like(hid_acc)
    out_acc[...] = jnp.zeros_like(out_acc)
    proj_acc[...] = jnp.zeros_like(proj_acc)
    for ref in (inters, acts, pre_cots):
        ref[...] = jnp.zeros_like(ref)
    for load in loads[2:]:
        load.wait()
    w1t_ref[...] = (w1_ref[...].T.astype(F32) * 0.5).astype(BF)
    w2h_ref[...] = (w2_ref[...].astype(F32) * 0.5).astype(BF)

    def act_cots(i, carry):
        for s in (2 * i, 2 * i + 1):
            act_cot[s] = nt(w2h_ref[...], c_ref[s])
        return carry

    lax.fori_loop(0, pairs, act_cots, 0)

    @pl.when(outer)
    def _():
        hear(0)
        tell(1)
        first_samples(6, 12)
        hear(1)
        first_samples(12, samples)

    def mlp(s, now, before):
        r = jnp.maximum(s - 1, 0)
        s = jnp.minimum(s, samples - 1)
        inter_cot = nn(w1_ref[...], pre_cots[before]).astype(BF)
        icot[r] = inter_cot
        inter = nt(full[0, s], e_ref[s]).astype(BF)
        hid_acc[...] += nt(inters[before], pre_cots[before])
        u = nn(w1t_ref[...], inter)
        out_acc[...] += nn(acts[before], c_ref[r])
        t = jnp.tanh(u)
        p = 1.0 + t
        a = u * p
        inters[now] = inter
        acts[now] = a.astype(BF)
        pre_cots[now] = (act_cot[s] * (p + a * (1.0 - t))).astype(BF)
        part[1, r] = nn(inter_cot, e_ref[r]).astype(BF)

    def grad_of(both):
        for s in both:
            total = tn(icot[s], full[0, s]) + nn(p_ref[...], full[1, s])
            eg_ref[s] = (c_ref[s].astype(F32) + total).astype(BF)

    def proj_of(own, both):
        emb = e_ref if own else e2_ref
        return sum(nt(full[1, s, mine], emb[s]) for s in both)

    def proj_some(both):
        for i in range(2):
            proj_acc[i] += proj_of(i == 0, both)

    def final(both):
        for s in both:
            share(1, s).wait_recv()
        grad_of(both)

    w_core = send(w_mine.at[:, 1 - c], w_buddy, wss.at[0], wrs.at[0], buddy)
    place = x * 4 + y
    w_xyc = []
    for d in range(1, 16):
        there = (place + d) % 16
        w_xyc.append(send(w_chip.at[there], w_xy.at[d], wss.at[1], wrs.at[1], (there * 2 + hi, ft)))
    w_xy_all = send(w_chip.at[pl.ds(0, 15)], w_xy.at[pl.ds(1, 15)], wss.at[1], wrs.at[1], buddy)
    slot = hi * 4 + z
    w_zc = [
        send(w_plane, w_z.at[slot], wss.at[2], wrs.at[2], (place * 2 + c, ((z + d) % 4) * 2 + c))
        for d in range(4)
    ]

    def w_z_some(count):
        return send(w_z.at[pl.ds(0, count)], w_z.at[pl.ds(0, count)], wss.at[2], wrs.at[2], buddy)

    w_last = send(w_all, w_all, wss.at[3], wrs.at[3], buddy)

    def w_first():
        hid = hid_acc[...].reshape(16, 2, 8, 512)
        hid = jnp.concatenate([hid[..., :256], hid[..., 256:]], axis=2)
        w_mine[..., :256] = hid.astype(BF)
        w_mine[..., 256:] = out_acc[...].reshape(16, 2, 16, 128).astype(BF)
        w_core.start()

    def w_along_xy():
        w_core.wait_recv()
        w_chip[...] = (w_mine[:, c].astype(F32) + w_buddy[...].astype(F32)).astype(BF)
        for copy in w_xyc:
            copy.start()

    def w_along_z():
        w_xy_all.wait_recv()
        total = w_chip[place].astype(F32)
        for d in range(1, 16):
            total += w_xy[d].astype(F32)
        w_plane[...] = total.astype(BF)
        for copy in w_zc[1:]:
            copy.start()

        @pl.when(c != hi)
        def _():
            w_zc[0].start()

        @pl.when(c == hi)
        def _():
            w_z[slot] = total.astype(BF)

    def w_share():
        @pl.when(c == hi)
        def _():
            w_z_some(7).wait_recv()
            total = w_z[0].astype(F32)
            for d in range(1, 8):
                total += w_z[d].astype(F32)
            w_all[...] = total
            w_last.start()

    def when(condition, act, *args):
        pl.when(condition)(lambda: act(*args))

    def within(u, lag, act, *args):
        when((u >= lag) & (u < lag + samples), act, *args, u - lag)

    lag_mlp = jnp.where(hub, LAG_MLP_HUB, LAG_MLP)

    def fill(u, carry):
        @pl.when(hub)
        def _():
            when(u == 0, hear, 0)
            when(u == 0, tell, 1)
            paired(0, u)
            when(u >= LAG_TOTAL, totalled, 0, u - LAG_TOTAL)

        when(outer & (u >= LAG_SHARE), shared, 0, u - LAG_SHARE)
        return carry

    def middle(s, carry):
        u = s + lag_mlp
        now = s % 2

        @pl.when(hub)
        def _():
            when(u == 8, hear, 1)
            within(u, 0, paired, 0)
            within(u, LAG_TOTAL, totalled, 0)

        when(s < samples, lambda: share(0, s).wait_recv())
        mlp(s, now, 1 - now)
        when(s > 0, lambda: to_buddy(1, s - 1).start())

        @pl.when(outer)
        def _():
            within(u, LAG_SHARE, shared, 0)
            when(s == 0, tell_ring, 2)
            when(s == 8, hear_ring, 2)
            when(s == 13, tell_ring, 3)
            within(u, LAG2_FIRST, first, 1)

        @pl.when(hub)
        def _():
            within(u, LAG2_PAIR, paired, 1)
            within(u, LAG2_TOTAL, totalled, 1)

        return carry

    def drain(u, carry):
        done = samples + lag_mlp + 1

        @pl.when(outer)
        def _():
            when(u == LAG2_FIRST + samples - 1, hear_ring, 3)
            within(u, LAG2_FIRST, first, 1)
            when(u >= LAG2_SHARE, shared, 1, u - LAG2_SHARE)

        @pl.when(hub)
        def _():
            within(u, LAG2_PAIR, paired, 1)
            within(u, LAG2_TOTAL, totalled, 1)

        when(u == done, w_first)
        when(u == done, swap.wait_recv)
        when(u == done + 3, w_along_xy)
        when(u == done + 10, w_along_z)
        s = u - LAG2_SHARE - 1

        @pl.when((s >= 0) & (s % 2 == 0))
        def _():
            proj_some([s, s + 1])

        return carry

    lax.fori_loop(0, lag_mlp, fill, 0)
    lax.fori_loop(0, samples + 1, middle, 0)
    lax.fori_loop(samples + lag_mlp + 1, samples - 2 + LAG2_SHARE, drain, 0)

    @pl.when(outer)
    def _():
        shared(1, samples - 2)

    proj_some([samples - 2])

    @pl.when(outer)
    def _():
        shared(1, samples - 1)

    here = p_land.at[pl.ds(dp, 1)]
    for i in range(2):
        proj = (proj_acc[i] + proj_of(i == 0, [samples - 1])).reshape(16, 8, 256)
        p_mine[i] = jnp.concatenate([proj[..., :128], proj[..., 128:]], axis=1).astype(BF)
    for dh, dy, xi, i in itertools.product((1, 0), (2, 1, 3, 0), (0, 1), (0, 1)):
        there = xi * 8 + ((y + dy) % 4) * 2 + (hi + dh) % 2
        core = c if i == 0 else 1 - c
        copy = send(p_mine.at[i, pl.ds(there, 1)], here, pss, prs, (half * 16 + there, z * 2 + core))
        if dh == 0 and dy == 0 and i == 0:
            pl.when(half * 2 + xi != x)(copy.start)
        else:
            copy.start()

    @pl.when(hi_half == half)
    def _():
        p_land[dp] = p_mine[0, dp % 16]

    def p_some(count):
        return send(p_land.at[pl.ds(0, count)], p_land.at[pl.ds(0, count)], pss, prs, buddy)

    def finals(i, carry):
        final([2 * i, 2 * i + 1])
        return carry

    lax.fori_loop(0, pairs // 2, finals, 0)
    w_share()
    lax.fori_loop(pairs // 2, pairs, finals, 0)

    for q in range(2):
        sent = [send(chip.at[q], land_b.at[q], ssem.at[q, k], rsem.at[q, 0, 0], buddy) for k in range(4)]
        for k in (0, 1, 3):
            sent[k].wait_send()

        @pl.when(hub)
        def _():
            sent[2].wait_send()
    w_core.wait_send()
    w_xy_all.wait_send()

    @pl.when(c != hi)
    def _():
        w_z_some(4).wait_send()
        w_last.wait_recv()

    @pl.when(c == hi)
    def _():
        w_z_some(3).wait_send()
        w_last.wait_send()

    hg_ref[:, :256] = w_all[:8, :256] * mlp_scale
    hg_ref[:, 256:] = w_all[8:, :256] * mlp_scale
    og_ref[...] = w_all[:, 256:] * mlp_scale
    pl.when(hi_half == half)(lambda: p_some(31).wait_recv())
    pl.when(hi_half != half)(lambda: p_some(32).wait_recv())
    total = p_land[0].astype(F32)
    for d in range(1, 32):
        total += p_land[d].astype(F32)
    pg_ref[:, :128] = total[:8] * proj_scale
    pg_ref[:, 128:] = total[8:] * proj_scale
    swap.wait_send()
    pl.when(hi_half == half)(lambda: p_some(31).wait_send())
    pl.when(hi_half != half)(lambda: p_some(32).wait_send())


def finish(*refs):
    count = (len(refs) - 1) // 2
    copies = [pltpu.make_async_copy(refs[i], refs[count + i], refs[-1].at[i]) for i in range(count)]
    for copy in copies:
        copy.start()
    for copy in copies:
        copy.wait()


def local(embeds, proj_weight, hidden_weight, out_weight, cotangent):
    n, f, d = embeds.shape
    k = proj_weight.shape[1]
    h = hidden_weight.shape[1]
    dp_count = lax.axis_size("dp")
    mlp_scale = 4.0 / (n * dp_count)
    proj_scale = 1.0 / (n * dp_count * math.sqrt(d))
    vmem = pltpu.VMEM
    dma = pltpu.SemaphoreType.DMA
    hbm = pl.BlockSpec(memory_space=pltpu.HBM)
    anywhere = pl.BlockSpec(memory_space=pl.ANY)
    inside = pl.BlockSpec(memory_space=pltpu.VMEM)
    shapes = (
        jax.ShapeDtypeStruct((n, f, d), BF),
        jax.ShapeDtypeStruct((8, f), F32),
        jax.ShapeDtypeStruct((8, h), F32),
        jax.ShapeDtypeStruct((16, d), F32),
    )
    results = pl.pallas_call(
        functools.partial(kernel, n, proj_scale, mlp_scale),
        out_shape=tuple(vmem(v.shape, v.dtype) for v in shapes),
        in_specs=[hbm] * 5,
        out_specs=(inside,) * 4,
        scratch_shapes=[
            vmem((n, f, d), BF), vmem((f, k), BF), vmem((k, h), BF), vmem((h, d), BF), vmem((n, f, d), BF),
            vmem((k, f), BF), vmem((h, k), BF), vmem((h, d), BF),
            vmem((2, n, k, d), BF),
            vmem((2, n, k // 2, d), BF),
            vmem((2, n, k // 2, d), BF),
            vmem((2, n, k // 2, d), BF),
            vmem((2, n, k // 2, d), BF),
            vmem((2, n, k // 2, d), BF),
            vmem((2, n, k, d), BF),
            vmem((n, h, f), F32),
            vmem((n, k, f), BF),
            vmem((2, k, f), BF), vmem((2, h, f), BF), vmem((2, h, f), BF),
            vmem((k, h), F32), vmem((h, d), F32), vmem((2, k // 2, f), F32),
            vmem((16, 2, 16, 384), BF), vmem((16, 16, 384), BF), vmem((16, 16, 384), BF),
            vmem((16, 16, 384), BF), vmem((16, 384), BF), vmem((8, 16, 384), BF), vmem((16, 384), F32),
            vmem((2, 16, 16, 128), BF), vmem((32, 16, 128), BF), vmem((n, f, d), BF),
            dma((5,)), dma((2, 5)), dma((2, n, 5)),
            dma((4,)), dma((4,)), dma, dma, pltpu.SemaphoreType.REGULAR((4,)),
        ],
        compiler_params=pltpu.CompilerParams(
            collective_id=0, has_side_effects=True, vmem_limit_bytes=48 * 1024 * 1024
        ),
    )(*[pltpu.with_memory_space_constraint(v, pltpu.HBM) for v in (embeds, proj_weight, hidden_weight, out_weight, cotangent)])
    grad, proj, hid, out = pl.pallas_call(
        finish,
        out_shape=shapes,
        in_specs=[inside] * 4,
        out_specs=(hbm,) * 4,
        scratch_shapes=[dma((4,))],
        compiler_params=pltpu.CompilerParams(vmem_limit_bytes=48 * 1024 * 1024),
    )(*results)
    return grad, proj.T, hid, out


def solution(mesh):
    placed = (P("dp", "feat", None), P("feat", None), P(), P(), P("dp", "feat", None))
    return jax.shard_map(
        local,
        mesh=mesh,
        in_specs=placed,
        out_specs=(P("dp", "feat", None), P("feat", "dp"), P("dp", None), P("dp", None)),
        check_vma=False,
    )
```
